256 devices in a mesh: lev: 4 (over x), var: 64 (over y, z, core).
Axes of the slice: x: 4, y: 4, z: 8, core: 2. Of those that a mesh axis runs over, the one named last changes fastest.
Arguments:
- ensemble: float32 [4, 128, 2048, 128], P('lev', 'var'), may hold values from -6 to 6
- obs_sites: int32 [4, 8], replicated, may hold values from 0 to 262143, as said below
- owner: int32 [4], replicated, may hold values from 0 to 255, as said below
- tile_mask: int32 [4, 64], replicated, may hold values from 0 to 1, as said below
- obs_values: float32 [4, 8], replicated, may hold values from -6 to 6
- obs_error: float32 [4, 8], replicated, may hold values from 0.2 to 2
Outputs:
- analysis: float32 [4, 128, 2048, 128], P('lev', 'var')
The draws below stay inside these ranges and needn't reach their ends.
Inputs may be any that keep to these rules, and one draw needn't show every extreme that they name: owner[b] // 64 is the level of block b's observations and owner[b] % 64 their tile. `obs_sites`: the 8 sites of a block are distinct, and each lies in the block's tile: site // 128 // 32 == owner[b] % 64. tile_mask[b, t] is 1 exactly where |t - owner[b] % 64| <= 3.
All inputs are finite; a program needn't handle non-finite values.
Results may differ from the reference program's by a relative error of at most 0.0001.
Values sent between devices are 32-bit elements; how exact they have to be, the bound alone decides.
A program may use at most 320 MiB of HBM per device.

```python
import math
import jax
import jax.numpy as jnp
from jax import lax

XS = 2048
YS = 128
M = 128
BLOCKS = 4
OBS = 8
LEVELS = 4
TILES = 64
XDEV = 32
RADIUS = 96
OWNERS = 256


def pick_owners(key):
    draw_key, place_key = jax.random.split(key)
    owners = jax.random.randint(draw_key, (BLOCKS,), 0, OWNERS)
    order = jax.random.permutation(place_key, BLOCKS)
    owners = owners.at[order[0]].set(OWNERS - 1)
    owners = owners.at[order[1]].set(0)
    return owners


def draw_owner(key, part):
    owners = pick_owners(key)
    return owners.astype(jnp.int32)


def sites_of_block(one_key, tile):
    perm_key, slot_key = jax.random.split(one_key)
    places = jax.random.permutation(perm_key, XDEV * YS)[:OBS]
    slot = jax.random.randint(slot_key, (), 0, OBS)
    target = jnp.where(tile == TILES - 1, XDEV * YS - 1, 0)
    needed = jnp.logical_or(tile == TILES - 1, tile == 0)
    present = jnp.any(places == target)
    forced = places.at[slot].set(target)
    return jnp.where(jnp.logical_and(needed, jnp.logical_not(present)), forced, places)


def draw_obs_sites(key, part):
    owners = pick_owners(key)
    key = jax.random.fold_in(key, 5)
    block_keys = jax.random.split(key, BLOCKS)
    tiles = owners % TILES
    places = jax.vmap(sites_of_block)(block_keys, tiles)
    across = tiles[:, None] * XDEV + places // YS
    return (across * YS + places % YS).astype(jnp.int32)


def draw_tile_mask(key, part):
    owners = pick_owners(key)
    tile_index = jnp.arange(TILES, dtype=jnp.int32)[None, :]
    return (jnp.abs(tile_index - (owners % TILES)[:, None]) <= 3).astype(jnp.int32)


def levels(rng, dims, cuts, least, top_value):
    factor_of, own = 1.0, jax.random.fold_in(rng, 6)
    for axis_at, blocks in cuts:
        draws = jnp.exp(jax.random.uniform(jax.random.fold_in(own, axis_at), (blocks,), jnp.float32, least / len(cuts), top_value / len(cuts)))
        factor_of = factor_of * jnp.repeat(draws, dims[axis_at] // blocks).reshape([-1 if axis == axis_at else 1 for axis in range(len(dims))])
    return factor_of


def gaussian(rng, dims, deviation, limit, cuts=(), kind=jnp.bfloat16):
    drawn = deviation * jax.random.normal(rng, dims, jnp.float32)
    if cuts:
        drawn = drawn * levels(rng, dims, cuts, -0.22, 0.18)
    return jnp.clip(drawn, -limit, limit).astype(kind)


def setup_inputs(seed: int = 0) -> dict:
    seeds = jax.random.split(jax.random.key(seed), 7)
    ensemble = gaussian(seeds[0], (LEVELS, M, XS, YS), 1.0, 6.0, ((0, 4), (1, 64)), jnp.float32)
    obs_sites = draw_obs_sites(jax.random.fold_in(seeds[6], 71), 0)
    owner = draw_owner(jax.random.fold_in(seeds[6], 71), 0)
    tile_mask = draw_tile_mask(jax.random.fold_in(seeds[6], 71), 0)
    obs_values = gaussian(seeds[4], (BLOCKS, OBS), 1.5, 6.0, (), jnp.float32)
    obs_error = jnp.clip(jnp.exp(jax.random.uniform(seeds[5], (BLOCKS, OBS), jnp.float32, math.log(0.2), math.log(2.0))), 0.2, 2.0)
    return dict(ensemble=ensemble, obs_sites=obs_sites, owner=owner, tile_mask=tile_mask, obs_values=obs_values, obs_error=obs_error)


def taper_weight(delta_x, delta_y, radius):
    return jnp.square(jnp.maximum(0.0, 1.0 - (delta_x * delta_x + delta_y * delta_y) / (radius * radius)))

def vertical(level_gap):
    return jnp.exp2(-jnp.abs(level_gap).astype(jnp.float32))

def obs_increment(current, observed, variance, members):
    centre = jnp.mean(current)
    anomaly = current - centre
    spread = jnp.sum(anomaly * anomaly) / (members - 1) + 1e-06
    shifts = spread / (spread + variance) * (observed - centre) + (jnp.sqrt(variance / (spread + variance)) - 1.0) * anomaly
    return (anomaly, shifts, (members - 1) * spread)

def reference(ensemble, obs_sites, owner, tile_mask, obs_values, obs_error):
    members = ensemble.shape[1]
    radius = jnp.float32(RADIUS)
    grid_x = jnp.arange(XS, dtype=jnp.int32).astype(jnp.float32)[:, None]
    grid_y = jnp.arange(YS, dtype=jnp.int32).astype(jnp.float32)[None, :]
    tile_of = jnp.arange(XS, dtype=jnp.int32) // XDEV
    level_ids = jnp.arange(LEVELS, dtype=jnp.int32)
    analysis = ensemble
    for block_no in range(BLOCKS):
        site_level = owner[block_no] // TILES
        site_x_int = obs_sites[block_no] // YS
        site_y_int = obs_sites[block_no] % YS
        level_slab = lax.dynamic_index_in_dim(analysis, site_level, 0, keepdims=False)
        priors = level_slab[:, site_x_int, site_y_int].T
        mask_row = tile_mask[block_no].astype(jnp.float32)
        row_mask = mask_row[site_x_int // XDEV]
        cell_mask = mask_row[tile_of]
        level_weight = vertical(level_ids - site_level)
        site_x = site_x_int.astype(jnp.float32)
        site_y = site_y_int.astype(jnp.float32)
        values = obs_values[block_no]
        errors = obs_error[block_no]

        def one_obs(obs_index, loop_state):
            priors, analysis = loop_state
            anomaly, shifts, scaled = obs_increment(priors[obs_index], values[obs_index], errors[obs_index], members)
            row_weight = row_mask * taper_weight(site_x - site_x[obs_index], site_y - site_y[obs_index], radius)
            regress = jnp.dot(priors, anomaly, precision=lax.Precision.HIGHEST)
            new_priors = priors + (row_weight * regress / scaled)[:, None] * shifts[None, :]
            cell_weight = level_weight[:, None, None] * cell_mask[None, :, None] * taper_weight(grid_x - site_x[obs_index], grid_y - site_y[obs_index], radius)[None]
            regress_cells = jnp.einsum('lmxy,m->lxy', analysis, anomaly, precision=lax.Precision.HIGHEST)
            new_analysis = analysis + (cell_weight * regress_cells / scaled)[:, None] * shifts[None, :, None, None]
            return (new_priors, new_analysis)
        priors, analysis = lax.fori_loop(0, OBS, one_obs, (priors, analysis))
    return analysis
```

```python
import functools

import jax
import jax.numpy as jnp
from jax import lax
from jax.experimental import pallas as pl
from jax.experimental.pallas import tpu as pltpu
from jax.sharding import PartitionSpec as P

MESH = pl.DeviceIdType.MESH
HIGHEST = lax.Precision.HIGHEST
F32 = jnp.float32
REACH = 3
HALF = 64


def step_at(value, edge):
    return jnp.minimum(jnp.maximum(value - edge + 1, 0), 1)


def changed_tiles(owner_ref, blocks, tiles, slots):
    t = [owner_ref[b] & (tiles - 1) for b in range(blocks)]
    for i in range(blocks):
        for j in range(blocks - 1 - i):
            t[j], t[j + 1] = jnp.minimum(t[j], t[j + 1]), jnp.maximum(t[j], t[j + 1])
    befores, gaps, total, end = [], [], 0, -1
    for b in range(blocks):
        start = jnp.maximum(jnp.maximum(t[b] - REACH, end + 1), 0)
        gaps.append(start - end - 1)
        end = jnp.minimum(t[b] + REACH, tiles - 1)
        befores.append(total)
        total = total + jnp.maximum(end - start + 1, 0)
    found = []
    for s in range(slots):
        tile = gaps[0] + s
        for b in range(1, blocks):
            tile = tile + gaps[b] * step_at(s, befores[b])
        found.append((tile + 1) * step_at(total - 1, s) - 1)
    return found


def taper(dx, dy, radius):
    return jnp.square(jnp.maximum(0.0, 1.0 - (dx * dx + dy * dy) / (radius * radius)))


def exchange_kernel(
    cfg,
    sites_ref,
    owner_ref,
    values_ref,
    errors_ref,
    ens_ref,
    back_ref,
    ens_v,
    out_buf,
    in_buf,
    ret_buf,
    site_v,
    near_buf,
    row_buf,
    row_in,
    wcol_v,
    wcell_v,
    hcol_v,
    r_v,
    load_sem,
    near_send,
    near_recv,
    row_send,
    row_recv,
    bulk_send,
    bulk_recv,
    ret_send,
    ret_recv,
    own_sem,
):
    levels, count, slots, tiles, width, blocks, obs = cfg
    n_obs = blocks * obs
    members = 2 * count
    lev = lax.axis_index("lev")
    me = lax.axis_index("var")
    radius = jnp.float32(REACH * width)
    tile_bits = tiles.bit_length() - 1

    barrier = pltpu.get_barrier_semaphore()

    def greet(j, carry):
        pl.semaphore_signal(
            barrier, inc=1, device_id=(lev, (me + j) % count), device_id_type=MESH
        )
        return carry

    lax.fori_loop(1, count, greet, 0)
    for j in range(1, levels):
        pl.semaphore_signal(
            barrier, inc=1, device_id=((lev + j) % levels, me), device_id_type=MESH
        )

    load = pltpu.make_async_copy(ens_ref, ens_v, load_sem)
    load.start()

    lane = lax.broadcasted_iota(jnp.int32, (1, 128), 1)
    low = lane < HALF
    tile_at = changed_tiles(owner_ref, blocks, tiles, slots)

    sub32 = lax.broadcasted_iota(jnp.int32, (n_obs, 128), 0)
    lane32 = lax.broadcasted_iota(jnp.int32, (n_obs, 128), 1)
    site_c = jnp.zeros((n_obs, 128), jnp.int32)
    own_c = jnp.zeros((n_obs, 128), jnp.int32)
    err_c = jnp.zeros((n_obs, 128), F32)
    val_c = jnp.zeros((n_obs, 128), F32)
    site_r = jnp.zeros((1, 128), jnp.int32)
    own_r = jnp.zeros((1, 128), jnp.int32)
    for i in range(n_obs):
        b, k = i // obs, i % obs
        at = sub32 == i
        site_c = jnp.where(at, sites_ref[b, k], site_c)
        own_c = jnp.where(at, owner_ref[b], own_c)
        err_c = jnp.where(at, errors_ref[b, k], err_c)
        val_c = jnp.where(at, values_ref[b, k], val_c)
        site_r = jnp.where(lane == i, sites_ref[b, k], site_r)
        own_r = jnp.where(lane == i, owner_ref[b], own_r)
    x_c = (site_c >> 7).astype(F32)
    y_c = (site_c & 127).astype(F32)
    t_c = own_c & (tiles - 1)
    l_c = own_c >> tile_bits
    x_r = (site_r >> 7).astype(F32)
    y_r = (site_r & 127).astype(F32)
    t_r = own_r & (tiles - 1)
    l_r = own_r >> tile_bits
    pair_w = (
        jnp.where(jnp.abs(t_c - t_r) <= REACH, 1.0, 0.0)
        * jnp.exp2(-jnp.abs(l_c - l_r).astype(F32))
        * taper(x_c - x_r, y_c - y_r, radius)
    )
    row_w = jnp.where((lane32 > sub32) & (lane32 < n_obs), pair_w, 0.0)
    for k in range(n_obs):
        b = k // obs
        site = sites_ref[b, k % obs]
        own = owner_ref[b]
        w = (
            jnp.where(jnp.abs(t_c - (own & (tiles - 1))) <= REACH, 1.0, 0.0)
            * jnp.exp2(-jnp.abs(l_c - (own >> tile_bits)).astype(F32))
            * taper(x_c - (site >> 7).astype(F32), y_c - (site & 127).astype(F32), radius)
        )
        wcol_v[k] = jnp.where(sub32 > k, w, 0.0)

    group, side, column = me // 16, (me // 8) % 2, me % 8
    cell_y = (side * HALF + lane % HALF).astype(F32)
    level_f = jnp.exp2(-jnp.abs(l_c - lev).astype(F32))
    for p in range(slots // 2):
        tile = jnp.where(low, tile_at[2 * p], tile_at[2 * p + 1])
        cell_x = (tile * width + group * 8 + column).astype(F32)
        inside = (tile >= 0) & (jnp.abs(t_c - tile) <= REACH)
        wcell_v[p] = (
            jnp.where(inside, 1.0, 0.0) * level_f * taper(cell_x - x_c, cell_y - y_c, radius)
        )

    load.wait()

    for m in range(2):
        for i in range(n_obs):
            b, k = i // obs, i % obs
            site = sites_ref[b, k]
            away = (owner_ref[b] >> tile_bits) - lev
            row = ens_v[m, site >> 10, pl.ds((site >> 7) & 7, 1), :]
            site_v[pl.ds(m * n_obs + i, 1), :] = jnp.where(
                lane == (site & 127) + 128 * away, row, 0.0
            )
    sums = jnp.sum(site_v[...], axis=1, keepdims=True)
    sub64 = lax.broadcasted_iota(jnp.int32, (2 * n_obs, 128), 0)
    lane64 = lax.broadcasted_iota(jnp.int32, (2 * n_obs, 128), 1)
    mine = jnp.sum(jnp.where(sub64 == lane64, sums, 0.0), axis=0, keepdims=True)
    near_buf[pl.ds(0, 8), :] = jnp.broadcast_to(mine, (8, 128))

    for s in range(slots):
        tile = jnp.maximum(tile_at[s], 0)
        for g in range(4):
            a = ens_v[0, tile * (width // 8) + g]
            c = ens_v[1, tile * (width // 8) + g]
            out_buf[pl.ds((g * 16) * slots + s, 8, stride=slots), :] = jnp.where(
                low, a, pltpu.roll(c, HALF, 1)
            )
            out_buf[pl.ds((g * 16 + 8) * slots + s, 8, stride=slots), :] = jnp.where(
                low, pltpu.roll(a, HALF, 1), c
            )

    pl.semaphore_wait(barrier, count - 1 + levels - 1)

    near = []
    for j in range(1, levels):
        copy = pltpu.make_async_remote_copy(
            near_buf.at[pl.ds(0, 8)],
            near_buf.at[pl.ds(8 * j, 8)],
            near_send.at[j],
            near_recv.at[j],
            device_id=((lev + j) % levels, me),
            device_id_type=MESH,
        )
        copy.start()
        near.append(copy)

    def send_out(j, carry):
        to = (me + j) % count
        pltpu.make_async_remote_copy(
            out_buf.at[pl.ds(to * slots, slots)],
            in_buf.at[pl.ds(me * slots, slots)],
            bulk_send,
            bulk_recv,
            device_id=(lev, to),
            device_id_type=MESH,
        ).start()
        return carry

    for copy in near:
        copy.wait_recv()
    row_buf[...] = (near_buf[pl.ds(0, 8), :] + near_buf[pl.ds(8, 8), :]) + (
        near_buf[pl.ds(16, 8), :] + near_buf[pl.ds(24, 8), :]
    )

    def send_row(j, carry):
        to = (me + j) % count
        pltpu.make_async_remote_copy(
            row_buf.at[pl.ds(0, 1)],
            row_in.at[pl.ds(me, 1)],
            row_send,
            row_recv,
            device_id=(lev, to),
            device_id_type=MESH,
        ).start()
        return carry

    lax.fori_loop(1, count, send_row, 0)
    lax.fori_loop(1, count, send_out, 0)
    row_in[pl.ds(me, 1), :] = row_buf[pl.ds(0, 1), :]
    in_buf[pl.ds(me * slots, slots), :] = out_buf[pl.ds(me * slots, slots), :]
    for copy in near:
        copy.wait_send()
    pltpu.make_async_copy(
        row_in.at[pl.ds(0, count - 1)], row_in.at[pl.ds(0, count - 1)], row_recv
    ).wait()

    raw = row_in[...]
    total = jnp.sum(raw, axis=0, keepdims=True)
    both = jnp.where(lane < n_obs, total + pltpu.roll(total, 128 - n_obs, 1), 0.0)
    mean_r = both / members
    mean2_r = mean_r + pltpu.roll(mean_r, n_obs, 1)
    centred = jnp.where(lane < 2 * n_obs, raw - mean2_r, 0.0)
    full = lax.dot_general(
        centred, centred, (((0,), (0,)), ((), ())), precision=HIGHEST, preferred_element_type=F32
    )
    gram = full[:n_obs] + pltpu.roll(full[n_obs : 2 * n_obs], 128 - n_obs, 1)
    gram = jnp.where(lane < n_obs, gram, 0.0)
    mean_c = jnp.sum(jnp.where(sub32 == lane32, mean_r, 0.0), axis=1, keepdims=True)
    mean_c = jnp.broadcast_to(mean_c, (n_obs, 128))
    mix = jnp.where(sub32 == lane32, 1.0, 0.0)
    alpha_c = jnp.zeros((n_obs, 128), F32)
    beta_c = jnp.zeros((n_obs, 128), F32)
    inv_c = jnp.zeros((n_obs, 128), F32)
    beta_r = jnp.zeros((1, 128), F32)
    for k in range(n_obs):
        u_row = gram[k : k + 1, :]
        u_col = jnp.broadcast_to(gram[:, k : k + 1], (n_obs, 128))
        d = u_col[k : k + 1, :]
        spread = d / (members - 1) + 1e-06
        r = err_c[k : k + 1, :]
        inv = 1.0 / (spread + r)
        alpha = spread * inv * (val_c[k : k + 1, :] - mean_c[k : k + 1, :])
        beta = jnp.sqrt(r * inv) - 1.0
        inv_scaled = 1.0 / ((members - 1) * spread)
        c_col = wcol_v[k] * u_col * inv_scaled
        g_row = row_w[k : k + 1, :] * u_row * (inv_scaled * beta)
        g_col = c_col * beta
        mean_c = mean_c + c_col * alpha
        gram = gram + (g_col * (u_row + g_row * d) + u_col * g_row)
        mix = mix + g_col * mix[k : k + 1, :]
        at = sub32 == k
        alpha_c = jnp.where(at, alpha, alpha_c)
        beta_c = jnp.where(at, beta, beta_c)
        inv_c = jnp.where(at, inv_scaled, inv_c)
        beta_r = jnp.where(lane == k, beta, beta_r)
    lower = jnp.where(lane32 < sub32, gram * beta_r, 0.0)
    for k in range(n_obs):
        hcol_v[k] = jnp.broadcast_to(lower[:, k : k + 1], (n_obs, 128))

    mix2 = jnp.concatenate([mix, pltpu.roll(mix, n_obs, 1)], axis=0)
    anomalies = lax.dot_general(
        mix2, centred, (((1,), (1,)), ((), ())), precision=HIGHEST, preferred_element_type=F32
    )
    shift = (
        jnp.concatenate([alpha_c, alpha_c], axis=0)[:, :count]
        + jnp.concatenate([beta_c, beta_c], axis=0)[:, :count] * anomalies
    )

    pltpu.make_async_copy(
        in_buf.at[pl.ds(0, (count - 1) * slots)],
        in_buf.at[pl.ds(0, (count - 1) * slots)],
        bulk_recv,
    ).wait()

    def half_sum(part):
        t = jnp.where(low, part[:n_obs], part[n_obs:])
        return t + pltpu.roll(t, HALF, 1)

    for p in range(slots // 2):
        x = jnp.concatenate(
            [
                in_buf[pl.ds(2 * p, count, stride=slots), :],
                in_buf[pl.ds(2 * p + 1, count, stride=slots), :],
            ],
            axis=1,
        )
        r2 = jnp.dot(anomalies, x, precision=HIGHEST, preferred_element_type=F32)
        r_v[p] = jnp.where(low, half_sum(r2[:, :128]), half_sum(r2[:, 128:]))

    for p in range(slots // 2):
        reg = r_v[p]
        w = wcell_v[p] * inv_c
        rows = []
        for k in range(n_obs):
            coef = w[k : k + 1, :] * reg[k : k + 1, :]
            rows.append(coef)
            if k + 1 < n_obs:
                reg = reg + hcol_v[k] * coef
        coefs = w * reg
        turned = pltpu.roll(coefs, HALF, 1)
        zero = jnp.zeros_like(coefs)
        first = jnp.concatenate(
            [jnp.where(low, coefs, zero), jnp.where(low, zero, turned)], axis=0
        )
        second = jnp.concatenate(
            [jnp.where(low, turned, zero), jnp.where(low, zero, coefs)], axis=0
        )
        delta = lax.dot_general(
            shift,
            jnp.concatenate([first, second], axis=1),
            (((0,), (0,)), ((), ())),
            precision=HIGHEST,
            preferred_element_type=F32,
        )
        ret_buf[pl.ds(2 * p, count, stride=slots), :] = delta[:, :128]
        ret_buf[pl.ds(2 * p + 1, count, stride=slots), :] = delta[:, 128:]

    def send_back(j, carry):
        to = (me + j) % count
        pltpu.make_async_remote_copy(
            ret_buf.at[pl.ds(to * slots, slots)],
            back_ref.at[pl.ds(me * slots, slots)],
            ret_send,
            ret_recv,
            device_id=(lev, to),
            device_id_type=MESH,
        ).start()
        return carry

    lax.fori_loop(1, count, send_back, 0)
    own = pltpu.make_async_copy(
        ret_buf.at[pl.ds(me * slots, slots)], back_ref.at[pl.ds(me * slots, slots)], own_sem
    )
    own.start()
    rest = pl.ds(0, (count - 1) * slots)
    pltpu.make_async_copy(row_in.at[pl.ds(0, count - 1)], row_in.at[pl.ds(0, count - 1)], row_send).wait()
    pltpu.make_async_copy(out_buf.at[rest], out_buf.at[rest], bulk_send).wait()
    own.wait()
    pltpu.make_async_copy(back_ref.at[rest], back_ref.at[rest], ret_recv).wait()
    pltpu.make_async_copy(ret_buf.at[rest], ret_buf.at[rest], ret_send).wait()


def apply_kernel(cfg, owner_ref, ens_ref, back_ref, out_ref, ens_v, back_v, sems):
    levels, count, slots, tiles, width, blocks, obs = cfg
    load = pltpu.make_async_copy(ens_ref, ens_v, sems.at[0])
    load_back = pltpu.make_async_copy(back_ref, back_v, sems.at[1])
    load_back.start()
    load.start()
    tile_at = changed_tiles(owner_ref, blocks, tiles, slots)
    low = lax.broadcasted_iota(jnp.int32, (1, 128), 1) < HALF
    load_back.wait()
    load.wait()
    for s in range(slots):
        tile = jnp.maximum(tile_at[s], 0)
        for g in range(4):
            a = back_v[pl.ds((g * 16) * slots + s, 8, stride=slots), :]
            c = back_v[pl.ds((g * 16 + 8) * slots + s, 8, stride=slots), :]
            at = tile * (width // 8) + g
            ens_v[0, at] = ens_v[0, at] + jnp.where(low, a, pltpu.roll(c, HALF, 1))
            ens_v[1, at] = ens_v[1, at] + jnp.where(low, pltpu.roll(a, HALF, 1), c)
    store = pltpu.make_async_copy(ens_v, out_ref, sems.at[2])
    store.start()
    store.wait()


def shards(slots, ensemble, obs_sites, owner, tile_mask, obs_values, obs_error):
    levels, count = lax.axis_size("lev"), lax.axis_size("var")
    _, m_dev, x_all, y_all = ensemble.shape
    tiles = tile_mask.shape[1]
    width = x_all // tiles
    blocks, obs = obs_sites.shape
    n_obs = blocks * obs
    cfg = (levels, count, slots, tiles, width, blocks, obs)
    ens = ensemble.reshape(m_dev, x_all // 8, 8, y_all)
    smem = pl.BlockSpec(memory_space=pltpu.SMEM)
    anywhere = pl.BlockSpec(memory_space=pl.ANY)
    dma = pltpu.SemaphoreType.DMA
    back = pl.pallas_call(
        functools.partial(exchange_kernel, cfg),
        out_shape=jax.ShapeDtypeStruct((count * slots, 128), F32),
        in_specs=[smem] * 4 + [anywhere],
        out_specs=anywhere,
        scratch_shapes=[
            pltpu.VMEM(ens.shape, F32),
            pltpu.VMEM((count * slots, 128), F32),
            pltpu.VMEM((count * slots, 128), F32),
            pltpu.VMEM((count * slots, 128), F32),
            pltpu.VMEM((2 * n_obs, 128), F32),
            pltpu.VMEM((8 * levels, 128), F32),
            pltpu.VMEM((8, 128), F32),
            pltpu.VMEM((count, 128), F32),
            pltpu.VMEM((n_obs, n_obs, 128), F32),
            pltpu.VMEM((slots // 2, n_obs, 128), F32),
            pltpu.VMEM((n_obs, n_obs, 128), F32),
            pltpu.VMEM((slots // 2, n_obs, 128), F32),
            dma,
            dma((levels,)),
            dma((levels,)),
            dma,
            dma,
            dma,
            dma,
            dma,
            dma,
            dma,
        ],
        compiler_params=pltpu.CompilerParams(
            collective_id=slots, has_side_effects=True, vmem_limit_bytes=40 * 2**20
        ),
    )(obs_sites, owner, obs_values, obs_error, ens)
    out = pl.pallas_call(
        functools.partial(apply_kernel, cfg),
        out_shape=jax.ShapeDtypeStruct(ens.shape, F32),
        in_specs=[smem, anywhere, anywhere],
        out_specs=anywhere,
        scratch_shapes=[
            pltpu.VMEM(ens.shape, F32),
            pltpu.VMEM((count * slots, 128), F32),
            dma((3,)),
        ],
        compiler_params=pltpu.CompilerParams(vmem_limit_bytes=40 * 2**20),
    )(owner, ens, back)
    return out.reshape(ensemble.shape)


def solution(mesh):
    in_specs = (P("lev", "var", None, None), P(), P(), P(), P(), P())
    out_specs = P("lev", "var", None, None)
    return jax.shard_map(
        functools.partial(shards, 32),
        mesh=mesh,
        in_specs=in_specs,
        out_specs=out_specs,
        check_vma=False,
    )
```

```python
import functools

import jax
import jax.numpy as jnp
from jax import lax
from jax.experimental import pallas as pl
from jax.experimental.pallas import tpu as pltpu
from jax.sharding import PartitionSpec as P

MESH = pl.DeviceIdType.MESH
HIGHEST = lax.Precision.HIGHEST
F32 = jnp.float32
REACH = 3
SIZES = (22, 28)
VMEM_BYTES = 64 * 2**20
HALF = 64


def step_at(value, edge):
    return jnp.minimum(jnp.maximum(value - edge + 1, 0), 1)


def changed_tiles(owner_ref, blocks, tiles, slots):
    t = [owner_ref[b] & (tiles - 1) for b in range(blocks)]
    for i in range(blocks):
        for j in range(blocks - 1 - i):
            t[j], t[j + 1] = jnp.minimum(t[j], t[j + 1]), jnp.maximum(t[j], t[j + 1])
    befores, gaps, total, end = [], [], 0, -1
    for b in range(blocks):
        start = jnp.maximum(jnp.maximum(t[b] - REACH, end + 1), 0)
        gaps.append(start - end - 1)
        end = jnp.minimum(t[b] + REACH, tiles - 1)
        befores.append(total)
        total = total + jnp.maximum(end - start + 1, 0)
    found = []
    for s in range(slots):
        tile = gaps[0] + s
        for b in range(1, blocks):
            tile = tile + gaps[b] * step_at(s, befores[b])
        found.append((tile + 1) * step_at(total - 1, s) - 1)
    return found


def taper(dx, dy, radius):
    return jnp.square(jnp.maximum(0.0, 1.0 - (dx * dx + dy * dy) / (radius * radius)))


def exchange_kernel(
    cfg,
    sites_hbm,
    owner_hbm,
    values_hbm,
    errors_hbm,
    ens_ref,
    back_ref,
    sites_ref,
    owner_ref,
    values_ref,
    errors_ref,
    ens_v,
    out_buf,
    in_buf,
    ret_buf,
    site_v,
    near_buf,
    row_buf,
    row_in,
    wcol_v,
    wcell_v,
    hcol_v,
    r_v,
    load_sem,
    small_sem,
    near_send,
    near_recv,
    row_send,
    row_recv,
    bulk_send,
    bulk_recv,
    ret_send,
    ret_recv,
    own_sem,
):
    levels, count, slots, tiles, width, blocks, obs = cfg
    n_obs = blocks * obs
    members = 2 * count
    lev = lax.axis_index("lev")
    me = lax.axis_index("var")
    radius = jnp.float32(REACH * width)
    tile_bits = tiles.bit_length() - 1

    load = pltpu.make_async_copy(ens_ref, ens_v, load_sem)
    small = [
        pltpu.make_async_copy(src, dst, small_sem.at[i])
        for i, (src, dst) in enumerate(
            [
                (owner_hbm, owner_ref),
                (sites_hbm, sites_ref),
                (values_hbm, values_ref),
                (errors_hbm, errors_ref),
            ]
        )
    ]
    for copy in small:
        copy.start()
    load.start()

    barrier = pltpu.get_barrier_semaphore()

    def greet(j, carry):
        pl.semaphore_signal(
            barrier, inc=1, device_id=(lev, (me + j) % count), device_id_type=MESH
        )
        return carry

    lax.fori_loop(1, count, greet, 0)
    for j in range(1, levels):
        pl.semaphore_signal(
            barrier, inc=1, device_id=((lev + j) % levels, me), device_id_type=MESH
        )

    for copy in small:
        copy.wait()

    lane = lax.broadcasted_iota(jnp.int32, (1, 128), 1)
    low = lane < HALF
    tile_at = changed_tiles(owner_ref, blocks, tiles, slots)

    sub32 = lax.broadcasted_iota(jnp.int32, (n_obs, 128), 0)
    lane32 = lax.broadcasted_iota(jnp.int32, (n_obs, 128), 1)
    site_c = jnp.zeros((n_obs, 128), jnp.int32)
    own_c = jnp.zeros((n_obs, 128), jnp.int32)
    err_c = jnp.zeros((n_obs, 128), F32)
    val_c = jnp.zeros((n_obs, 128), F32)
    site_r = jnp.zeros((1, 128), jnp.int32)
    own_r = jnp.zeros((1, 128), jnp.int32)
    for i in range(n_obs):
        b, k = i // obs, i % obs
        at = sub32 == i
        site_c = jnp.where(at, sites_ref[b, k], site_c)
        own_c = jnp.where(at, owner_ref[b], own_c)
        err_c = jnp.where(at, errors_ref[b, k], err_c)
        val_c = jnp.where(at, values_ref[b, k], val_c)
        site_r = jnp.where(lane == i, sites_ref[b, k], site_r)
        own_r = jnp.where(lane == i, owner_ref[b], own_r)
    x_c = (site_c >> 7).astype(F32)
    y_c = (site_c & 127).astype(F32)
    t_c = own_c & (tiles - 1)
    l_c = own_c >> tile_bits
    x_r = (site_r >> 7).astype(F32)
    y_r = (site_r & 127).astype(F32)
    t_r = own_r & (tiles - 1)
    l_r = own_r >> tile_bits
    pair_w = (
        jnp.where(jnp.abs(t_c - t_r) <= REACH, 1.0, 0.0)
        * jnp.exp2(-jnp.abs(l_c - l_r).astype(F32))
        * taper(x_c - x_r, y_c - y_r, radius)
    )
    row_w = jnp.where((lane32 > sub32) & (lane32 < n_obs), pair_w, 0.0)
    for k in range(n_obs):
        b = k // obs
        site = sites_ref[b, k % obs]
        own = owner_ref[b]
        w = (
            jnp.where(jnp.abs(t_c - (own & (tiles - 1))) <= REACH, 1.0, 0.0)
            * jnp.exp2(-jnp.abs(l_c - (own >> tile_bits)).astype(F32))
            * taper(x_c - (site >> 7).astype(F32), y_c - (site & 127).astype(F32), radius)
        )
        wcol_v[k] = jnp.where(sub32 > k, w, 0.0)

    group, side, column = me // 16, (me // 8) % 2, me % 8
    cell_y = (side * HALF + lane % HALF).astype(F32)
    level_f = jnp.exp2(-jnp.abs(l_c - lev).astype(F32))
    for p in range(slots // 2):
        tile = jnp.where(low, tile_at[2 * p], tile_at[2 * p + 1])
        cell_x = (tile * width + group * 8 + column).astype(F32)
        inside = (tile >= 0) & (jnp.abs(t_c - tile) <= REACH)
        wcell_v[p] = (
            jnp.where(inside, 1.0, 0.0) * level_f * taper(cell_x - x_c, cell_y - y_c, radius)
        )

    load.wait()

    for m in range(2):
        for i in range(n_obs):
            b, k = i // obs, i % obs
            site = sites_ref[b, k]
            away = (owner_ref[b] >> tile_bits) - lev
            row = ens_v[m, site >> 10, pl.ds((site >> 7) & 7, 1), :]
            site_v[pl.ds(m * n_obs + i, 1), :] = jnp.where(
                lane == (site & 127) + 128 * away, row, 0.0
            )
    sums = jnp.sum(site_v[...], axis=1, keepdims=True)
    sub64 = lax.broadcasted_iota(jnp.int32, (2 * n_obs, 128), 0)
    lane64 = lax.broadcasted_iota(jnp.int32, (2 * n_obs, 128), 1)
    mine = jnp.sum(jnp.where(sub64 == lane64, sums, 0.0), axis=0, keepdims=True)
    near_buf[pl.ds(0, 8), :] = jnp.broadcast_to(mine, (8, 128))

    for s in range(slots):
        tile = jnp.maximum(tile_at[s], 0)
        for g in range(4):
            a = ens_v[0, tile * (width // 8) + g]
            c = ens_v[1, tile * (width // 8) + g]
            out_buf[pl.ds((g * 16) * slots + s, 8, stride=slots), :] = jnp.where(
                low, a, pltpu.roll(c, HALF, 1)
            )
            out_buf[pl.ds((g * 16 + 8) * slots + s, 8, stride=slots), :] = jnp.where(
                low, pltpu.roll(a, HALF, 1), c
            )

    pl.semaphore_wait(barrier, count - 1 + levels - 1)

    near = []
    for j in range(1, levels):
        copy = pltpu.make_async_remote_copy(
            near_buf.at[pl.ds(0, 8)],
            near_buf.at[pl.ds(8 * j, 8)],
            near_send.at[j],
            near_recv.at[j],
            device_id=((lev + j) % levels, me),
            device_id_type=MESH,
        )
        copy.start()
        near.append(copy)

    def send_out(j, carry):
        to = (me + j) % count
        pltpu.make_async_remote_copy(
            out_buf.at[pl.ds(to * slots, slots)],
            in_buf.at[pl.ds(me * slots, slots)],
            bulk_send,
            bulk_recv,
            device_id=(lev, to),
            device_id_type=MESH,
        ).start()
        return carry

    for copy in near:
        copy.wait_recv()
    row_buf[...] = (near_buf[pl.ds(0, 8), :] + near_buf[pl.ds(8, 8), :]) + (
        near_buf[pl.ds(16, 8), :] + near_buf[pl.ds(24, 8), :]
    )

    def send_row(j, carry):
        to = (me + j) % count
        pltpu.make_async_remote_copy(
            row_buf.at[pl.ds(0, 1)],
            row_in.at[pl.ds(me, 1)],
            row_send,
            row_recv,
            device_id=(lev, to),
            device_id_type=MESH,
        ).start()
        return carry

    lax.fori_loop(1, count, send_row, 0)
    lax.fori_loop(1, count, send_out, 0)
    row_in[pl.ds(me, 1), :] = row_buf[pl.ds(0, 1), :]
    in_buf[pl.ds(me * slots, slots), :] = out_buf[pl.ds(me * slots, slots), :]
    for copy in near:
        copy.wait_send()
    pltpu.make_async_copy(
        row_in.at[pl.ds(0, count - 1)], row_in.at[pl.ds(0, count - 1)], row_recv
    ).wait()

    raw = row_in[...]
    total = jnp.sum(raw, axis=0, keepdims=True)
    both = jnp.where(lane < n_obs, total + pltpu.roll(total, 128 - n_obs, 1), 0.0)
    mean_r = both / members
    mean2_r = mean_r + pltpu.roll(mean_r, n_obs, 1)
    centred = jnp.where(lane < 2 * n_obs, raw - mean2_r, 0.0)
    full = lax.dot_general(
        centred, centred, (((0,), (0,)), ((), ())), precision=HIGHEST, preferred_element_type=F32
    )
    gram = full[:n_obs] + pltpu.roll(full[n_obs : 2 * n_obs], 128 - n_obs, 1)
    gram = jnp.where(lane < n_obs, gram, 0.0)
    mean_c = jnp.sum(jnp.where(sub32 == lane32, mean_r, 0.0), axis=1, keepdims=True)
    mean_c = jnp.broadcast_to(mean_c, (n_obs, 128))
    mix = jnp.where(sub32 == lane32, 1.0, 0.0)
    alpha_c = jnp.zeros((n_obs, 128), F32)
    beta_c = jnp.zeros((n_obs, 128), F32)
    inv_c = jnp.zeros((n_obs, 128), F32)
    beta_r = jnp.zeros((1, 128), F32)
    for k in range(n_obs):
        u_row = gram[k : k + 1, :]
        u_col = jnp.broadcast_to(gram[:, k : k + 1], (n_obs, 128))
        d = u_col[k : k + 1, :]
        spread = d / (members - 1) + 1e-06
        r = err_c[k : k + 1, :]
        inv = 1.0 / (spread + r)
        alpha = spread * inv * (val_c[k : k + 1, :] - mean_c[k : k + 1, :])
        beta = jnp.sqrt(r * inv) - 1.0
        inv_scaled = 1.0 / ((members - 1) * spread)
        c_col = wcol_v[k] * u_col * inv_scaled
        g_row = row_w[k : k + 1, :] * u_row * (inv_scaled * beta)
        g_col = c_col * beta
        mean_c = mean_c + c_col * alpha
        gram = gram + (g_col * (u_row + g_row * d) + u_col * g_row)
        mix = mix + g_col * mix[k : k + 1, :]
        at = sub32 == k
        alpha_c = jnp.where(at, alpha, alpha_c)
        beta_c = jnp.where(at, beta, beta_c)
        inv_c = jnp.where(at, inv_scaled, inv_c)
        beta_r = jnp.where(lane == k, beta, beta_r)
    lower = jnp.where(lane32 < sub32, gram * beta_r, 0.0)
    for k in range(n_obs):
        hcol_v[k] = jnp.broadcast_to(lower[:, k : k + 1], (n_obs, 128))

    mix2 = jnp.concatenate([mix, pltpu.roll(mix, n_obs, 1)], axis=0)
    anomalies = lax.dot_general(
        mix2, centred, (((1,), (1,)), ((), ())), precision=HIGHEST, preferred_element_type=F32
    )
    shift = (
        jnp.concatenate([alpha_c, alpha_c], axis=0)[:, :count]
        + jnp.concatenate([beta_c, beta_c], axis=0)[:, :count] * anomalies
    )

    pltpu.make_async_copy(
        in_buf.at[pl.ds(0, (count - 1) * slots)],
        in_buf.at[pl.ds(0, (count - 1) * slots)],
        bulk_recv,
    ).wait()

    def half_sum(part):
        t = jnp.where(low, part[:n_obs], part[n_obs:])
        return t + pltpu.roll(t, HALF, 1)

    for p in range(slots // 2):
        x = jnp.concatenate(
            [
                in_buf[pl.ds(2 * p, count, stride=slots), :],
                in_buf[pl.ds(2 * p + 1, count, stride=slots), :],
            ],
            axis=1,
        )
        r2 = jnp.dot(anomalies, x, precision=HIGHEST, preferred_element_type=F32)
        r_v[p] = jnp.where(low, half_sum(r2[:, :128]), half_sum(r2[:, 128:]))

    for p in range(slots // 2):
        reg = r_v[p]
        w = wcell_v[p] * inv_c
        rows = []
        for k in range(n_obs):
            coef = w[k : k + 1, :] * reg[k : k + 1, :]
            rows.append(coef)
            if k + 1 < n_obs:
                reg = reg + hcol_v[k] * coef
        coefs = w * reg
        turned = pltpu.roll(coefs, HALF, 1)
        zero = jnp.zeros_like(coefs)
        first = jnp.concatenate(
            [jnp.where(low, coefs, zero), jnp.where(low, zero, turned)], axis=0
        )
        second = jnp.concatenate(
            [jnp.where(low, turned, zero), jnp.where(low, zero, coefs)], axis=0
        )
        delta = lax.dot_general(
            shift,
            jnp.concatenate([first, second], axis=1),
            (((0,), (0,)), ((), ())),
            precision=HIGHEST,
            preferred_element_type=F32,
        )
        ret_buf[pl.ds(2 * p, count, stride=slots), :] = delta[:, :128]
        ret_buf[pl.ds(2 * p + 1, count, stride=slots), :] = delta[:, 128:]

    def send_back(j, carry):
        to = (me + j) % count
        pltpu.make_async_remote_copy(
            ret_buf.at[pl.ds(to * slots, slots)],
            back_ref.at[pl.ds(me * slots, slots)],
            ret_send,
            ret_recv,
            device_id=(lev, to),
            device_id_type=MESH,
        ).start()
        return carry

    lax.fori_loop(1, count, send_back, 0)
    own = pltpu.make_async_copy(
        ret_buf.at[pl.ds(me * slots, slots)], back_ref.at[pl.ds(me * slots, slots)], own_sem
    )
    own.start()
    rest = pl.ds(0, (count - 1) * slots)
    pltpu.make_async_copy(row_in.at[pl.ds(0, count - 1)], row_in.at[pl.ds(0, count - 1)], row_send).wait()
    pltpu.make_async_copy(out_buf.at[rest], out_buf.at[rest], bulk_send).wait()
    own.wait()
    pltpu.make_async_copy(back_ref.at[rest], back_ref.at[rest], ret_recv).wait()
    pltpu.make_async_copy(ret_buf.at[rest], ret_buf.at[rest], ret_send).wait()


def apply_kernel(cfg, owner_hbm, ens_ref, back_ref, out_ref, owner_ref, ens_v, back_v, sems):
    levels, count, slots, tiles, width, blocks, obs = cfg
    small = pltpu.make_async_copy(owner_hbm, owner_ref, sems.at[0])
    small.start()
    load_back = pltpu.make_async_copy(back_ref, back_v, sems.at[1])
    load_back.start()
    loads = [
        pltpu.make_async_copy(ens_ref.at[m], ens_v.at[m], sems.at[2 + m]) for m in range(2)
    ]
    for load in loads:
        load.start()
    small.wait()
    tile_at = [jnp.maximum(t, 0) for t in changed_tiles(owner_ref, blocks, tiles, slots)]
    low = lax.broadcasted_iota(jnp.int32, (1, 128), 1) < HALF
    load_back.wait()
    stores = []
    for m in range(2):
        loads[m].wait()
        for s in range(slots):
            for g in range(4):
                a = back_v[pl.ds((g * 16) * slots + s, 8, stride=slots), :]
                c = back_v[pl.ds((g * 16 + 8) * slots + s, 8, stride=slots), :]
                at = tile_at[s] * (width // 8) + g
                if m == 0:
                    added = jnp.where(low, a, pltpu.roll(c, HALF, 1))
                else:
                    added = jnp.where(low, pltpu.roll(a, HALF, 1), c)
                ens_v[m, at] = ens_v[m, at] + added
        store = pltpu.make_async_copy(ens_v.at[m], out_ref.at[m], sems.at[4 + m])
        store.start()
        stores.append(store)
    for store in stores:
        store.wait()


def filter_tiles(cfg, ens, obs_sites, owner, obs_values, obs_error):
    levels, count, slots, tiles, width, blocks, obs = cfg
    n_obs = blocks * obs
    hbm = pl.BlockSpec(memory_space=pltpu.HBM)
    anywhere = pl.BlockSpec(memory_space=pl.ANY)
    dma = pltpu.SemaphoreType.DMA
    limit = VMEM_BYTES - 4 * count * slots * 128
    back = pl.pallas_call(
        functools.partial(exchange_kernel, cfg),
        out_shape=jax.ShapeDtypeStruct((count * slots, 128), F32),
        in_specs=[hbm] * 5,
        out_specs=anywhere,
        scratch_shapes=[
            pltpu.SMEM(obs_sites.shape, jnp.int32),
            pltpu.SMEM(owner.shape, jnp.int32),
            pltpu.SMEM(obs_values.shape, F32),
            pltpu.SMEM(obs_error.shape, F32),
            pltpu.VMEM(ens.shape, F32),
            pltpu.VMEM((count * slots, 128), F32),
            pltpu.VMEM((count * slots, 128), F32),
            pltpu.VMEM((count * slots, 128), F32),
            pltpu.VMEM((2 * n_obs, 128), F32),
            pltpu.VMEM((8 * levels, 128), F32),
            pltpu.VMEM((8, 128), F32),
            pltpu.VMEM((count, 128), F32),
            pltpu.VMEM((n_obs, n_obs, 128), F32),
            pltpu.VMEM((slots // 2, n_obs, 128), F32),
            pltpu.VMEM((n_obs, n_obs, 128), F32),
            pltpu.VMEM((slots // 2, n_obs, 128), F32),
            dma,
            dma((4,)),
            dma((levels,)),
            dma((levels,)),
            dma,
            dma,
            dma,
            dma,
            dma,
            dma,
            dma,
        ],
        compiler_params=pltpu.CompilerParams(
            collective_id=slots, has_side_effects=True, vmem_limit_bytes=limit
        ),
    )(obs_sites, owner, obs_values, obs_error, ens)
    return pl.pallas_call(
        functools.partial(apply_kernel, cfg),
        out_shape=jax.ShapeDtypeStruct(ens.shape, F32),
        in_specs=[hbm, hbm, anywhere],
        out_specs=hbm,
        scratch_shapes=[
            pltpu.SMEM(owner.shape, jnp.int32),
            pltpu.VMEM(ens.shape, F32),
            pltpu.VMEM((count * slots, 128), F32),
            dma((6,)),
        ],
        compiler_params=pltpu.CompilerParams(vmem_limit_bytes=limit),
    )(owner, ens, back)


def shards(sizes, ensemble, obs_sites, owner, tile_mask, obs_values, obs_error):
    levels, count = lax.axis_size("lev"), lax.axis_size("var")
    _, m_dev, x_all, y_all = ensemble.shape
    blocks, obs = obs_sites.shape
    tiles = tile_mask.shape[1]
    ens = ensemble.reshape(m_dev, x_all // 8, 8, y_all)
    rest = (ens, obs_sites, owner, obs_values, obs_error)
    branches = [
        functools.partial(filter_tiles, (levels, count, n, tiles, x_all // tiles, blocks, obs))
        for n in sizes
    ]
    if len(sizes) == 1:
        out = branches[0](*rest)
    else:
        touched = jnp.sum(jnp.max(tile_mask, axis=0))
        which = sum((touched > n).astype(jnp.int32) for n in sizes[:-1])
        out = lax.switch(which, branches, *rest)
    return out.reshape(ensemble.shape)


def solution(mesh):
    in_specs = (P("lev", "var", None, None), P(), P(), P(), P(), P())
    out_specs = P("lev", "var", None, None)
    return jax.shard_map(
        functools.partial(shards, SIZES),
        mesh=mesh,
        in_specs=in_specs,
        out_specs=out_specs,
        check_vma=False,
    )
```

```python
import functools

import jax
import jax.numpy as jnp
from jax import lax
from jax.experimental import pallas as pl
from jax.experimental.pallas import tpu as pltpu
from jax.sharding import PartitionSpec as P

MESH = pl.DeviceIdType.MESH
HIGHEST = lax.Precision.HIGHEST
F32 = jnp.float32
REACH = 3
SIZES = (22, 28)
EARLY = 32
VMEM_BYTES = 64 * 2**20
HALF = 64


def step_at(value, edge):
    return jnp.minimum(jnp.maximum(value - edge + 1, 0), 1)


def changed_tiles(owner_ref, blocks, tiles, slots):
    t = [owner_ref[b] & (tiles - 1) for b in range(blocks)]
    for i in range(blocks):
        for j in range(blocks - 1 - i):
            t[j], t[j + 1] = jnp.minimum(t[j], t[j + 1]), jnp.maximum(t[j], t[j + 1])
    befores, gaps, total, end = [], [], 0, -1
    for b in range(blocks):
        start = jnp.maximum(jnp.maximum(t[b] - REACH, end + 1), 0)
        gaps.append(start - end - 1)
        end = jnp.minimum(t[b] + REACH, tiles - 1)
        befores.append(total)
        total = total + jnp.maximum(end - start + 1, 0)
    found = []
    for s in range(slots):
        tile = gaps[0] + s
        for b in range(1, blocks):
            tile = tile + gaps[b] * step_at(s, befores[b])
        found.append((tile + 1) * step_at(total - 1, s) - 1)
    return found


def taper(dx, dy, radius):
    return jnp.square(jnp.maximum(0.0, 1.0 - (dx * dx + dy * dy) / (radius * radius)))


def exchange_kernel(
    cfg,
    sites_hbm,
    owner_hbm,
    values_hbm,
    errors_hbm,
    ens_ref,
    back_ref,
    sites_ref,
    owner_ref,
    values_ref,
    errors_ref,
    ens_v,
    out_buf,
    in_buf,
    ret_buf,
    site_v,
    near_buf,
    row_buf,
    row_in,
    wcol_v,
    wcell_v,
    hcol_v,
    r_v,
    load_sem,
    small_sem,
    near_send,
    near_recv,
    row_send,
    row_recv,
    bulk_send,
    bulk_recv,
    ret_send,
    ret_recv,
    own_sem,
):
    levels, count, slots, tiles, width, blocks, obs = cfg
    n_obs = blocks * obs
    members = 2 * count
    lev = lax.axis_index("lev")
    me = lax.axis_index("var")
    radius = jnp.float32(REACH * width)
    tile_bits = tiles.bit_length() - 1

    load = pltpu.make_async_copy(ens_ref, ens_v, load_sem)
    small = [
        pltpu.make_async_copy(src, dst, small_sem.at[i])
        for i, (src, dst) in enumerate(
            [
                (owner_hbm, owner_ref),
                (sites_hbm, sites_ref),
                (values_hbm, values_ref),
                (errors_hbm, errors_ref),
            ]
        )
    ]
    for copy in small:
        copy.start()
    load.start()

    barrier = pltpu.get_barrier_semaphore()

    def greet(j, carry):
        pl.semaphore_signal(
            barrier, inc=1, device_id=(lev, lax.rem(me + j, count)), device_id_type=MESH
        )
        return carry

    lax.fori_loop(1, count, greet, 0)
    for j in range(1, levels):
        pl.semaphore_signal(
            barrier, inc=1, device_id=((lev + j) % levels, me), device_id_type=MESH
        )

    for copy in small:
        copy.wait()

    lane = lax.broadcasted_iota(jnp.int32, (1, 128), 1)
    low = lane < HALF
    tile_at = changed_tiles(owner_ref, blocks, tiles, slots)

    load.wait()

    for m in range(2):
        for i in range(n_obs):
            b, k = i // obs, i % obs
            site = sites_ref[b, k]
            away = (owner_ref[b] >> tile_bits) - lev
            row = ens_v[m, site >> 10, pl.ds((site >> 7) & 7, 1), :]
            site_v[pl.ds(m * n_obs + i, 1), :] = jnp.where(
                lane == (site & 127) + 128 * away, row, 0.0
            )
    sums = jnp.sum(site_v[...], axis=1, keepdims=True)
    sub64 = lax.broadcasted_iota(jnp.int32, (2 * n_obs, 128), 0)
    lane64 = lax.broadcasted_iota(jnp.int32, (2 * n_obs, 128), 1)
    mine = jnp.sum(jnp.where(sub64 == lane64, sums, 0.0), axis=0, keepdims=True)
    near_buf[pl.ds(0, 8), :] = jnp.broadcast_to(mine, (8, 128))

    for s in range(slots):
        tile = jnp.maximum(tile_at[s], 0)
        for g in range(4):
            a = ens_v[0, tile * (width // 8) + g]
            c = ens_v[1, tile * (width // 8) + g]
            out_buf[pl.ds((g * 16) * slots + s, 8, stride=slots), :] = jnp.where(
                low, a, pltpu.roll(c, HALF, 1)
            )
            out_buf[pl.ds((g * 16 + 8) * slots + s, 8, stride=slots), :] = jnp.where(
                low, pltpu.roll(a, HALF, 1), c
            )

    pl.semaphore_wait(barrier, count - 1 + levels - 1)

    near = []
    for j in range(1, levels):
        copy = pltpu.make_async_remote_copy(
            near_buf.at[pl.ds(0, 8)],
            near_buf.at[pl.ds(8 * j, 8)],
            near_send.at[j],
            near_recv.at[j],
            device_id=((lev + j) % levels, me),
            device_id_type=MESH,
        )
        copy.start()
        near.append(copy)

    def send_out(j, carry):
        to = lax.rem(me + j, count)
        pltpu.make_async_remote_copy(
            out_buf.at[pl.ds(to * slots, slots)],
            in_buf.at[pl.ds(me * slots, slots)],
            bulk_send,
            bulk_recv,
            device_id=(lev, to),
            device_id_type=MESH,
        ).start()
        return carry

    lax.fori_loop(1, EARLY, send_out, 0)
    for copy in near:
        copy.wait_recv()
    row_buf[...] = (near_buf[pl.ds(0, 8), :] + near_buf[pl.ds(8, 8), :]) + (
        near_buf[pl.ds(16, 8), :] + near_buf[pl.ds(24, 8), :]
    )

    def send_row(j, carry):
        to = lax.rem(me + j, count)
        pltpu.make_async_remote_copy(
            row_buf.at[pl.ds(0, 1)],
            row_in.at[pl.ds(me, 1)],
            row_send,
            row_recv,
            device_id=(lev, to),
            device_id_type=MESH,
        ).start()
        return carry

    lax.fori_loop(1, count, send_row, 0)
    lax.fori_loop(EARLY, count, send_out, 0)
    row_in[pl.ds(me, 1), :] = row_buf[pl.ds(0, 1), :]
    in_buf[pl.ds(me * slots, slots), :] = out_buf[pl.ds(me * slots, slots), :]
    sub32 = lax.broadcasted_iota(jnp.int32, (n_obs, 128), 0)
    lane32 = lax.broadcasted_iota(jnp.int32, (n_obs, 128), 1)
    site_c = jnp.zeros((n_obs, 128), jnp.int32)
    own_c = jnp.zeros((n_obs, 128), jnp.int32)
    err_c = jnp.zeros((n_obs, 128), F32)
    val_c = jnp.zeros((n_obs, 128), F32)
    site_r = jnp.zeros((1, 128), jnp.int32)
    own_r = jnp.zeros((1, 128), jnp.int32)
    for i in range(n_obs):
        b, k = i // obs, i % obs
        at = sub32 == i
        site_c = jnp.where(at, sites_ref[b, k], site_c)
        own_c = jnp.where(at, owner_ref[b], own_c)
        err_c = jnp.where(at, errors_ref[b, k], err_c)
        val_c = jnp.where(at, values_ref[b, k], val_c)
        site_r = jnp.where(lane == i, sites_ref[b, k], site_r)
        own_r = jnp.where(lane == i, owner_ref[b], own_r)
    x_c = (site_c >> 7).astype(F32)
    y_c = (site_c & 127).astype(F32)
    t_c = own_c & (tiles - 1)
    l_c = own_c >> tile_bits
    x_r = (site_r >> 7).astype(F32)
    y_r = (site_r & 127).astype(F32)
    t_r = own_r & (tiles - 1)
    l_r = own_r >> tile_bits
    pair_w = (
        jnp.where(jnp.abs(t_c - t_r) <= REACH, 1.0, 0.0)
        * jnp.exp2(-jnp.abs(l_c - l_r).astype(F32))
        * taper(x_c - x_r, y_c - y_r, radius)
    )
    row_w = jnp.where((lane32 > sub32) & (lane32 < n_obs), pair_w, 0.0)
    for k in range(n_obs):
        b = k // obs
        site = sites_ref[b, k % obs]
        own = owner_ref[b]
        w = (
            jnp.where(jnp.abs(t_c - (own & (tiles - 1))) <= REACH, 1.0, 0.0)
            * jnp.exp2(-jnp.abs(l_c - (own >> tile_bits)).astype(F32))
            * taper(x_c - (site >> 7).astype(F32), y_c - (site & 127).astype(F32), radius)
        )
        wcol_v[k] = jnp.where(sub32 > k, w, 0.0)

    group, side, column = me // 16, (me // 8) % 2, me % 8
    cell_y = (side * HALF + lane % HALF).astype(F32)
    level_f = jnp.exp2(-jnp.abs(l_c - lev).astype(F32))
    for p in range(slots // 2):
        tile = jnp.where(low, tile_at[2 * p], tile_at[2 * p + 1])
        cell_x = (tile * width + group * 8 + column).astype(F32)
        inside = (tile >= 0) & (jnp.abs(t_c - tile) <= REACH)
        wcell_v[p] = (
            jnp.where(inside, 1.0, 0.0) * level_f * taper(cell_x - x_c, cell_y - y_c, radius)
        )

    for copy in near:
        copy.wait_send()
    pltpu.make_async_copy(
        row_in.at[pl.ds(0, count - 1)], row_in.at[pl.ds(0, count - 1)], row_recv
    ).wait()

    raw = row_in[...]
    total = jnp.sum(raw, axis=0, keepdims=True)
    both = jnp.where(lane < n_obs, total + pltpu.roll(total, 128 - n_obs, 1), 0.0)
    mean_r = both / members
    mean2_r = mean_r + pltpu.roll(mean_r, n_obs, 1)
    centred = jnp.where(lane < 2 * n_obs, raw - mean2_r, 0.0)
    full = lax.dot_general(
        centred, centred, (((0,), (0,)), ((), ())), precision=HIGHEST, preferred_element_type=F32
    )
    gram = full[:n_obs] + pltpu.roll(full[n_obs : 2 * n_obs], 128 - n_obs, 1)
    gram = jnp.where(lane < n_obs, gram, 0.0)
    mean_c = jnp.sum(jnp.where(sub32 == lane32, mean_r, 0.0), axis=1, keepdims=True)
    mean_c = jnp.broadcast_to(mean_c, (n_obs, 128))
    mix = jnp.where(sub32 == lane32, 1.0, 0.0)
    alpha_c = jnp.zeros((n_obs, 128), F32)
    beta_c = jnp.zeros((n_obs, 128), F32)
    inv_c = jnp.zeros((n_obs, 128), F32)
    beta_r = jnp.zeros((1, 128), F32)
    for k in range(n_obs):
        u_row = gram[k : k + 1, :]
        u_col = jnp.broadcast_to(gram[:, k : k + 1], (n_obs, 128))
        d = u_col[k : k + 1, :]
        spread = d / (members - 1) + 1e-06
        r = err_c[k : k + 1, :]
        inv = 1.0 / (spread + r)
        alpha = spread * inv * (val_c[k : k + 1, :] - mean_c[k : k + 1, :])
        beta = jnp.sqrt(r * inv) - 1.0
        inv_scaled = 1.0 / ((members - 1) * spread)
        c_col = wcol_v[k] * u_col * inv_scaled
        g_row = row_w[k : k + 1, :] * u_row * (inv_scaled * beta)
        g_col = c_col * beta
        mean_c = mean_c + c_col * alpha
        gram = gram + (g_col * (u_row + g_row * d) + u_col * g_row)
        mix = mix + g_col * mix[k : k + 1, :]
        at = sub32 == k
        alpha_c = jnp.where(at, alpha, alpha_c)
        beta_c = jnp.where(at, beta, beta_c)
        inv_c = jnp.where(at, inv_scaled, inv_c)
        beta_r = jnp.where(lane == k, beta, beta_r)
    lower = jnp.where(lane32 < sub32, gram * beta_r, 0.0)
    for k in range(n_obs):
        hcol_v[k] = jnp.broadcast_to(lower[:, k : k + 1], (n_obs, 128))

    mix2 = jnp.concatenate([mix, pltpu.roll(mix, n_obs, 1)], axis=0)
    anomalies = lax.dot_general(
        mix2, centred, (((1,), (1,)), ((), ())), precision=HIGHEST, preferred_element_type=F32
    )
    shift = (
        jnp.concatenate([alpha_c, alpha_c], axis=0)[:, :count]
        + jnp.concatenate([beta_c, beta_c], axis=0)[:, :count] * anomalies
    )

    pltpu.make_async_copy(
        in_buf.at[pl.ds(0, (count - 1) * slots)],
        in_buf.at[pl.ds(0, (count - 1) * slots)],
        bulk_recv,
    ).wait()

    def half_sum(part):
        t = jnp.where(low, part[:n_obs], part[n_obs:])
        return t + pltpu.roll(t, HALF, 1)

    for p in range(slots // 2):
        x = jnp.concatenate(
            [
                in_buf[pl.ds(2 * p, count, stride=slots), :],
                in_buf[pl.ds(2 * p + 1, count, stride=slots), :],
            ],
            axis=1,
        )
        r2 = jnp.dot(anomalies, x, precision=HIGHEST, preferred_element_type=F32)
        r_v[p] = jnp.where(low, half_sum(r2[:, :128]), half_sum(r2[:, 128:]))

    for p in range(slots // 2):
        reg = r_v[p]
        w = wcell_v[p] * inv_c
        rows = []
        for k in range(n_obs):
            coef = w[k : k + 1, :] * reg[k : k + 1, :]
            rows.append(coef)
            if k + 1 < n_obs:
                reg = reg + hcol_v[k] * coef
        coefs = w * reg
        turned = pltpu.roll(coefs, HALF, 1)
        zero = jnp.zeros_like(coefs)
        first = jnp.concatenate(
            [jnp.where(low, coefs, zero), jnp.where(low, zero, turned)], axis=0
        )
        second = jnp.concatenate(
            [jnp.where(low, turned, zero), jnp.where(low, zero, coefs)], axis=0
        )
        delta = lax.dot_general(
            shift,
            jnp.concatenate([first, second], axis=1),
            (((0,), (0,)), ((), ())),
            precision=HIGHEST,
            preferred_element_type=F32,
        )
        ret_buf[pl.ds(2 * p, count, stride=slots), :] = delta[:, :128]
        ret_buf[pl.ds(2 * p + 1, count, stride=slots), :] = delta[:, 128:]

    def send_back(j, carry):
        to = lax.rem(me + j, count)
        pltpu.make_async_remote_copy(
            ret_buf.at[pl.ds(to * slots, slots)],
            back_ref.at[pl.ds(me * slots, slots)],
            ret_send,
            ret_recv,
            device_id=(lev, to),
            device_id_type=MESH,
        ).start()
        return carry

    lax.fori_loop(1, count, send_back, 0)
    own = pltpu.make_async_copy(
        ret_buf.at[pl.ds(me * slots, slots)], back_ref.at[pl.ds(me * slots, slots)], own_sem
    )
    own.start()
    rest = pl.ds(0, (count - 1) * slots)
    pltpu.make_async_copy(row_in.at[pl.ds(0, count - 1)], row_in.at[pl.ds(0, count - 1)], row_send).wait()
    pltpu.make_async_copy(out_buf.at[rest], out_buf.at[rest], bulk_send).wait()
    own.wait()
    pltpu.make_async_copy(back_ref.at[rest], back_ref.at[rest], ret_recv).wait()
    pltpu.make_async_copy(ret_buf.at[rest], ret_buf.at[rest], ret_send).wait()


def apply_kernel(cfg, owner_hbm, ens_ref, back_ref, out_ref, owner_ref, ens_v, back_v, sems):
    levels, count, slots, tiles, width, blocks, obs = cfg
    small = pltpu.make_async_copy(owner_hbm, owner_ref, sems.at[0])
    small.start()
    load_back = pltpu.make_async_copy(back_ref, back_v, sems.at[1])
    load_back.start()
    loads = [
        pltpu.make_async_copy(ens_ref.at[m], ens_v.at[m], sems.at[2 + m]) for m in range(2)
    ]
    for load in loads:
        load.start()
    small.wait()
    tile_at = [jnp.maximum(t, 0) for t in changed_tiles(owner_ref, blocks, tiles, slots)]
    low = lax.broadcasted_iota(jnp.int32, (1, 128), 1) < HALF
    load_back.wait()
    stores = []
    for m in range(2):
        loads[m].wait()
        for s in range(slots):
            for g in range(4):
                a = back_v[pl.ds((g * 16) * slots + s, 8, stride=slots), :]
                c = back_v[pl.ds((g * 16 + 8) * slots + s, 8, stride=slots), :]
                at = tile_at[s] * (width // 8) + g
                if m == 0:
                    added = jnp.where(low, a, pltpu.roll(c, HALF, 1))
                else:
                    added = jnp.where(low, pltpu.roll(a, HALF, 1), c)
                ens_v[m, at] = ens_v[m, at] + added
        store = pltpu.make_async_copy(ens_v.at[m], out_ref.at[m], sems.at[4 + m])
        store.start()
        stores.append(store)
    for store in stores:
        store.wait()


def filter_tiles(cfg, ens, obs_sites, owner, obs_values, obs_error):
    levels, count, slots, tiles, width, blocks, obs = cfg
    n_obs = blocks * obs
    hbm = pl.BlockSpec(memory_space=pltpu.HBM)
    anywhere = pl.BlockSpec(memory_space=pl.ANY)
    dma = pltpu.SemaphoreType.DMA
    limit = VMEM_BYTES - 4 * count * slots * 128
    back = pl.pallas_call(
        functools.partial(exchange_kernel, cfg),
        out_shape=jax.ShapeDtypeStruct((count * slots, 128), F32),
        in_specs=[hbm] * 5,
        out_specs=anywhere,
        scratch_shapes=[
            pltpu.SMEM(obs_sites.shape, jnp.int32),
            pltpu.SMEM(owner.shape, jnp.int32),
            pltpu.SMEM(obs_values.shape, F32),
            pltpu.SMEM(obs_error.shape, F32),
            pltpu.VMEM(ens.shape, F32),
            pltpu.VMEM((count * slots, 128), F32),
            pltpu.VMEM((count * slots, 128), F32),
            pltpu.VMEM((count * slots, 128), F32),
            pltpu.VMEM((2 * n_obs, 128), F32),
            pltpu.VMEM((8 * levels, 128), F32),
            pltpu.VMEM((8, 128), F32),
            pltpu.VMEM((count, 128), F32),
            pltpu.VMEM((n_obs, n_obs, 128), F32),
            pltpu.VMEM((slots // 2, n_obs, 128), F32),
            pltpu.VMEM((n_obs, n_obs, 128), F32),
            pltpu.VMEM((slots // 2, n_obs, 128), F32),
            dma,
            dma((4,)),
            dma((levels,)),
            dma((levels,)),
            dma,
            dma,
            dma,
            dma,
            dma,
            dma,
            dma,
        ],
        compiler_params=pltpu.CompilerParams(
            collective_id=slots, has_side_effects=True, vmem_limit_bytes=limit
        ),
    )(obs_sites, owner, obs_values, obs_error, ens)
    return pl.pallas_call(
        functools.partial(apply_kernel, cfg),
        out_shape=jax.ShapeDtypeStruct(ens.shape, F32),
        in_specs=[hbm, hbm, anywhere],
        out_specs=hbm,
        scratch_shapes=[
            pltpu.SMEM(owner.shape, jnp.int32),
            pltpu.VMEM(ens.shape, F32),
            pltpu.VMEM((count * slots, 128), F32),
            dma((6,)),
        ],
        compiler_params=pltpu.CompilerParams(vmem_limit_bytes=limit),
    )(owner, ens, back)


def shards(sizes, ensemble, obs_sites, owner, tile_mask, obs_values, obs_error):
    levels, count = lax.axis_size("lev"), lax.axis_size("var")
    _, m_dev, x_all, y_all = ensemble.shape
    blocks, obs = obs_sites.shape
    tiles = tile_mask.shape[1]
    ens = ensemble.reshape(m_dev, x_all // 8, 8, y_all)
    rest = (ens, obs_sites, owner, obs_values, obs_error)
    branches = [
        functools.partial(filter_tiles, (levels, count, n, tiles, x_all // tiles, blocks, obs))
        for n in sizes
    ]
    if len(sizes) == 1:
        out = branches[0](*rest)
    else:
        touched = jnp.sum(jnp.max(tile_mask, axis=0))
        which = sum((touched > n).astype(jnp.int32) for n in sizes[:-1])
        out = lax.switch(which, branches, *rest)
    return out.reshape(ensemble.shape)


def solution(mesh):
    in_specs = (P("lev", "var", None, None), P(), P(), P(), P(), P())
    out_specs = P("lev", "var", None, None)
    return jax.shard_map(
        functools.partial(shards, SIZES),
        mesh=mesh,
        in_specs=in_specs,
        out_specs=out_specs,
        check_vma=False,
    )
```

```python
import functools

import jax
import jax.numpy as jnp
from jax import lax
from jax.experimental import pallas as pl
from jax.experimental.pallas import tpu as pltpu
from jax.sharding import PartitionSpec as P

MESH = pl.DeviceIdType.MESH
HIGHEST = lax.Precision.HIGHEST
F32 = jnp.float32
REACH = 3
LAYOUTS = ((8, 14), (10, 18))
VMEM_BYTES = 64 * 2**20
HALF = 64


def step_at(value, edge):
    return jnp.minimum(jnp.maximum(value - edge + 1, 0), 1)


def changed_tiles(owner_ref, blocks, tiles, slots):
    t = [owner_ref[b] & (tiles - 1) for b in range(blocks)]
    for i in range(blocks):
        for j in range(blocks - 1 - i):
            t[j], t[j + 1] = jnp.minimum(t[j], t[j + 1]), jnp.maximum(t[j], t[j + 1])
    befores, gaps, total, end = [], [], 0, -1
    for b in range(blocks):
        start = jnp.maximum(jnp.maximum(t[b] - REACH, end + 1), 0)
        gaps.append(start - end - 1)
        end = jnp.minimum(t[b] + REACH, tiles - 1)
        befores.append(total)
        total = total + jnp.maximum(end - start + 1, 0)
    found = []
    for s in range(slots):
        tile = gaps[0] + s
        for b in range(1, blocks):
            tile = tile + gaps[b] * step_at(s, befores[b])
        found.append((tile + 1) * step_at(total - 1, s) - 1)
    return found


def places(parts, count):
    firsts = [sum(parts[:p]) for p in range(len(parts))]
    return firsts, [count * first for first in firsts]


def taper(dx, dy, radius):
    return jnp.square(jnp.maximum(0.0, 1.0 - (dx * dx + dy * dy) / (radius * radius)))


def exchange_kernel(
    cfg,
    sites_hbm,
    owner_hbm,
    values_hbm,
    errors_hbm,
    ens_ref,
    back_ref,
    sites_ref,
    owner_ref,
    values_ref,
    errors_ref,
    ens_v,
    out_buf,
    in_buf,
    ret_buf,
    site_v,
    near_buf,
    row_buf,
    row_in,
    wcol_v,
    wcell_v,
    hcol_v,
    r_v,
    load_sem,
    small_sem,
    near_send,
    near_recv,
    row_send,
    row_recv,
    bulk_send,
    bulk_recv,
    ret_send,
    ret_recv,
    own_sem,
):
    levels, count, parts, tiles, width, blocks, obs = cfg
    slots = sum(parts)
    n_obs = blocks * obs
    members = 2 * count
    lev = lax.axis_index("lev")
    me = lax.axis_index("var")
    radius = jnp.float32(REACH * width)
    tile_bits = tiles.bit_length() - 1
    firsts, bases = places(parts, count)

    load = pltpu.make_async_copy(ens_ref, ens_v, load_sem)
    small = [
        pltpu.make_async_copy(src, dst, small_sem.at[i])
        for i, (src, dst) in enumerate(
            [
                (owner_hbm, owner_ref),
                (sites_hbm, sites_ref),
                (values_hbm, values_ref),
                (errors_hbm, errors_ref),
            ]
        )
    ]
    for copy in small:
        copy.start()
    load.start()

    barrier = pltpu.get_barrier_semaphore()

    def greet(j, carry):
        pl.semaphore_signal(
            barrier, inc=1, device_id=(lev, lax.rem(me + j, count)), device_id_type=MESH
        )
        return carry

    lax.fori_loop(1, count, greet, 0)
    for j in range(1, levels):
        pl.semaphore_signal(
            barrier, inc=1, device_id=((lev + j) % levels, me), device_id_type=MESH
        )

    for copy in small:
        copy.wait()

    lane = lax.broadcasted_iota(jnp.int32, (1, 128), 1)
    low = lane < HALF
    tile_at = changed_tiles(owner_ref, blocks, tiles, slots)

    load.wait()

    for m in range(2):
        for i in range(n_obs):
            b, k = i // obs, i % obs
            site = sites_ref[b, k]
            away = (owner_ref[b] >> tile_bits) - lev
            row = ens_v[m, site >> 10, pl.ds((site >> 7) & 7, 1), :]
            site_v[pl.ds(m * n_obs + i, 1), :] = jnp.where(
                lane == (site & 127) + 128 * away, row, 0.0
            )
    sums = jnp.sum(site_v[...], axis=1, keepdims=True)
    sub64 = lax.broadcasted_iota(jnp.int32, (2 * n_obs, 128), 0)
    lane64 = lax.broadcasted_iota(jnp.int32, (2 * n_obs, 128), 1)
    mine = jnp.sum(jnp.where(sub64 == lane64, sums, 0.0), axis=0, keepdims=True)
    near_buf[pl.ds(0, 8), :] = jnp.broadcast_to(mine, (8, 128))

    for p, size in enumerate(parts):
        for r in range(size):
            tile = jnp.maximum(tile_at[firsts[p] + r], 0)
            for g in range(4):
                a = ens_v[0, tile * (width // 8) + g]
                c = ens_v[1, tile * (width // 8) + g]
                row = bases[p] + g * 16 * size + r
                out_buf[pl.ds(row, 8, stride=size), :] = jnp.where(low, a, pltpu.roll(c, HALF, 1))
                out_buf[pl.ds(row + 8 * size, 8, stride=size), :] = jnp.where(
                    low, pltpu.roll(a, HALF, 1), c
                )

    pl.semaphore_wait(barrier, count - 1 + levels - 1)

    near = []
    for j in range(1, levels):
        copy = pltpu.make_async_remote_copy(
            near_buf.at[pl.ds(0, 8)],
            near_buf.at[pl.ds(8 * j, 8)],
            near_send.at[j],
            near_recv.at[j],
            device_id=((lev + j) % levels, me),
            device_id_type=MESH,
        )
        copy.start()
        near.append(copy)

    def send_part(p, src, dst, send_sem, recv_sem):
        size = parts[p]

        def send(j, carry):
            to = lax.rem(me + j, count)
            pltpu.make_async_remote_copy(
                src.at[pl.ds(bases[p] + to * size, size)],
                dst.at[pl.ds(bases[p] + me * size, size)],
                send_sem.at[p],
                recv_sem.at[p],
                device_id=(lev, to),
                device_id_type=MESH,
            ).start()
            return carry

        lax.fori_loop(1, count, send, 0)

    def wait_part(p, buf, sem):
        rest = pl.ds(bases[p], (count - 1) * parts[p])
        pltpu.make_async_copy(buf.at[rest], buf.at[rest], sem.at[p]).wait()

    send_part(0, out_buf, in_buf, bulk_send, bulk_recv)
    for copy in near:
        copy.wait_recv()
    row_buf[...] = (near_buf[pl.ds(0, 8), :] + near_buf[pl.ds(8, 8), :]) + (
        near_buf[pl.ds(16, 8), :] + near_buf[pl.ds(24, 8), :]
    )

    def send_row(j, carry):
        to = lax.rem(me + j, count)
        pltpu.make_async_remote_copy(
            row_buf.at[pl.ds(0, 1)],
            row_in.at[pl.ds(me, 1)],
            row_send,
            row_recv,
            device_id=(lev, to),
            device_id_type=MESH,
        ).start()
        return carry

    lax.fori_loop(1, count, send_row, 0)
    for p in range(1, len(parts)):
        send_part(p, out_buf, in_buf, bulk_send, bulk_recv)
    row_in[pl.ds(me, 1), :] = row_buf[pl.ds(0, 1), :]
    for p, size in enumerate(parts):
        here = pl.ds(bases[p] + me * size, size)
        in_buf[here, :] = out_buf[here, :]
    sub32 = lax.broadcasted_iota(jnp.int32, (n_obs, 128), 0)
    lane32 = lax.broadcasted_iota(jnp.int32, (n_obs, 128), 1)
    site_c = jnp.zeros((n_obs, 128), jnp.int32)
    own_c = jnp.zeros((n_obs, 128), jnp.int32)
    err_c = jnp.zeros((n_obs, 128), F32)
    val_c = jnp.zeros((n_obs, 128), F32)
    site_r = jnp.zeros((1, 128), jnp.int32)
    own_r = jnp.zeros((1, 128), jnp.int32)
    for i in range(n_obs):
        b, k = i // obs, i % obs
        at = sub32 == i
        site_c = jnp.where(at, sites_ref[b, k], site_c)
        own_c = jnp.where(at, owner_ref[b], own_c)
        err_c = jnp.where(at, errors_ref[b, k], err_c)
        val_c = jnp.where(at, values_ref[b, k], val_c)
        site_r = jnp.where(lane == i, sites_ref[b, k], site_r)
        own_r = jnp.where(lane == i, owner_ref[b], own_r)
    x_c = (site_c >> 7).astype(F32)
    y_c = (site_c & 127).astype(F32)
    t_c = own_c & (tiles - 1)
    l_c = own_c >> tile_bits
    x_r = (site_r >> 7).astype(F32)
    y_r = (site_r & 127).astype(F32)
    t_r = own_r & (tiles - 1)
    l_r = own_r >> tile_bits
    pair_w = (
        jnp.where(jnp.abs(t_c - t_r) <= REACH, 1.0, 0.0)
        * jnp.exp2(-jnp.abs(l_c - l_r).astype(F32))
        * taper(x_c - x_r, y_c - y_r, radius)
    )
    row_w = jnp.where((lane32 > sub32) & (lane32 < n_obs), pair_w, 0.0)
    for k in range(n_obs):
        b = k // obs
        site = sites_ref[b, k % obs]
        own = owner_ref[b]
        w = (
            jnp.where(jnp.abs(t_c - (own & (tiles - 1))) <= REACH, 1.0, 0.0)
            * jnp.exp2(-jnp.abs(l_c - (own >> tile_bits)).astype(F32))
            * taper(x_c - (site >> 7).astype(F32), y_c - (site & 127).astype(F32), radius)
        )
        wcol_v[k] = jnp.where(sub32 > k, w, 0.0)

    group, side, column = me // 16, (me // 8) % 2, me % 8
    cell_y = (side * HALF + lane % HALF).astype(F32)
    level_f = jnp.exp2(-jnp.abs(l_c - lev).astype(F32))
    for p in range(slots // 2):
        tile = jnp.where(low, tile_at[2 * p], tile_at[2 * p + 1])
        cell_x = (tile * width + group * 8 + column).astype(F32)
        inside = (tile >= 0) & (jnp.abs(t_c - tile) <= REACH)
        wcell_v[p] = (
            jnp.where(inside, 1.0, 0.0) * level_f * taper(cell_x - x_c, cell_y - y_c, radius)
        )

    for copy in near:
        copy.wait_send()
    pltpu.make_async_copy(
        row_in.at[pl.ds(0, count - 1)], row_in.at[pl.ds(0, count - 1)], row_recv
    ).wait()

    raw = row_in[...]
    total = jnp.sum(raw, axis=0, keepdims=True)
    both = jnp.where(lane < n_obs, total + pltpu.roll(total, 128 - n_obs, 1), 0.0)
    mean_r = both / members
    mean2_r = mean_r + pltpu.roll(mean_r, n_obs, 1)
    centred = jnp.where(lane < 2 * n_obs, raw - mean2_r, 0.0)
    full = lax.dot_general(
        centred, centred, (((0,), (0,)), ((), ())), precision=HIGHEST, preferred_element_type=F32
    )
    gram = full[:n_obs] + pltpu.roll(full[n_obs : 2 * n_obs], 128 - n_obs, 1)
    gram = jnp.where(lane < n_obs, gram, 0.0)
    mean_c = jnp.sum(jnp.where(sub32 == lane32, mean_r, 0.0), axis=1, keepdims=True)
    mean_c = jnp.broadcast_to(mean_c, (n_obs, 128))
    mix = jnp.where(sub32 == lane32, 1.0, 0.0)
    alpha_c = jnp.zeros((n_obs, 128), F32)
    beta_c = jnp.zeros((n_obs, 128), F32)
    inv_c = jnp.zeros((n_obs, 128), F32)
    beta_r = jnp.zeros((1, 128), F32)
    for k in range(n_obs):
        u_row = gram[k : k + 1, :]
        u_col = jnp.broadcast_to(gram[:, k : k + 1], (n_obs, 128))
        d = u_col[k : k + 1, :]
        spread = d / (members - 1) + 1e-06
        r = err_c[k : k + 1, :]
        inv = 1.0 / (spread + r)
        alpha = spread * inv * (val_c[k : k + 1, :] - mean_c[k : k + 1, :])
        beta = jnp.sqrt(r * inv) - 1.0
        inv_scaled = 1.0 / ((members - 1) * spread)
        c_col = wcol_v[k] * u_col * inv_scaled
        g_row = row_w[k : k + 1, :] * u_row * (inv_scaled * beta)
        g_col = c_col * beta
        mean_c = mean_c + c_col * alpha
        gram = gram + (g_col * (u_row + g_row * d) + u_col * g_row)
        mix = mix + g_col * mix[k : k + 1, :]
        at = sub32 == k
        alpha_c = jnp.where(at, alpha, alpha_c)
        beta_c = jnp.where(at, beta, beta_c)
        inv_c = jnp.where(at, inv_scaled, inv_c)
        beta_r = jnp.where(lane == k, beta, beta_r)
    lower = jnp.where(lane32 < sub32, gram * beta_r, 0.0)
    for k in range(n_obs):
        hcol_v[k] = jnp.broadcast_to(lower[:, k : k + 1], (n_obs, 128))

    mix2 = jnp.concatenate([mix, pltpu.roll(mix, n_obs, 1)], axis=0)
    anomalies = lax.dot_general(
        mix2, centred, (((1,), (1,)), ((), ())), precision=HIGHEST, preferred_element_type=F32
    )
    shift = (
        jnp.concatenate([alpha_c, alpha_c], axis=0)[:, :count]
        + jnp.concatenate([beta_c, beta_c], axis=0)[:, :count] * anomalies
    )

    def half_sum(part):
        t = jnp.where(low, part[:n_obs], part[n_obs:])
        return t + pltpu.roll(t, HALF, 1)

    own = []
    for p, size in enumerate(parts):
        wait_part(p, in_buf, bulk_recv)
        for q in range(size // 2):
            row = bases[p] + 2 * q
            x = jnp.concatenate(
                [
                    in_buf[pl.ds(row, count, stride=size), :],
                    in_buf[pl.ds(row + 1, count, stride=size), :],
                ],
                axis=1,
            )
            r2 = jnp.dot(anomalies, x, precision=HIGHEST, preferred_element_type=F32)
            r_v[firsts[p] // 2 + q] = jnp.where(low, half_sum(r2[:, :128]), half_sum(r2[:, 128:]))

        for q in range(size // 2):
            row = bases[p] + 2 * q
            reg = r_v[firsts[p] // 2 + q]
            w = wcell_v[firsts[p] // 2 + q] * inv_c
            for k in range(n_obs - 1):
                reg = reg + hcol_v[k] * (w[k : k + 1, :] * reg[k : k + 1, :])
            coefs = w * reg
            turned = pltpu.roll(coefs, HALF, 1)
            zero = jnp.zeros_like(coefs)
            first = jnp.concatenate(
                [jnp.where(low, coefs, zero), jnp.where(low, zero, turned)], axis=0
            )
            second = jnp.concatenate(
                [jnp.where(low, turned, zero), jnp.where(low, zero, coefs)], axis=0
            )
            delta = lax.dot_general(
                shift,
                jnp.concatenate([first, second], axis=1),
                (((0,), (0,)), ((), ())),
                precision=HIGHEST,
                preferred_element_type=F32,
            )
            ret_buf[pl.ds(row, count, stride=size), :] = delta[:, :128]
            ret_buf[pl.ds(row + 1, count, stride=size), :] = delta[:, 128:]

        send_part(p, ret_buf, back_ref, ret_send, ret_recv)
        here = pl.ds(bases[p] + me * size, size)
        copy = pltpu.make_async_copy(ret_buf.at[here], back_ref.at[here], own_sem.at[p])
        copy.start()
        own.append(copy)

    rows = row_in.at[pl.ds(0, count - 1)]
    pltpu.make_async_copy(rows, rows, row_send).wait()
    for p in range(len(parts)):
        wait_part(p, out_buf, bulk_send)
        own[p].wait()
    for p in range(len(parts)):
        wait_part(p, back_ref, ret_recv)
    for p in range(len(parts)):
        wait_part(p, ret_buf, ret_send)


def apply_kernel(cfg, owner_hbm, ens_ref, back_ref, out_ref, owner_ref, ens_v, back_v, sems):
    levels, count, parts, tiles, width, blocks, obs = cfg
    slots = sum(parts)
    small = pltpu.make_async_copy(owner_hbm, owner_ref, sems.at[0])
    small.start()
    firsts, bases = places(parts, count)
    load_back = pltpu.make_async_copy(back_ref, back_v, sems.at[1])
    load_back.start()
    loads = [
        pltpu.make_async_copy(ens_ref.at[m], ens_v.at[m], sems.at[2 + m]) for m in range(2)
    ]
    for load in loads:
        load.start()
    small.wait()
    tile_at = [jnp.maximum(t, 0) for t in changed_tiles(owner_ref, blocks, tiles, slots)]
    low = lax.broadcasted_iota(jnp.int32, (1, 128), 1) < HALF
    load_back.wait()
    stores = []
    for m in range(2):
        loads[m].wait()
        for p, size in enumerate(parts):
            for r in range(size):
                for g in range(4):
                    row = bases[p] + g * 16 * size + r
                    a = back_v[pl.ds(row, 8, stride=size), :]
                    c = back_v[pl.ds(row + 8 * size, 8, stride=size), :]
                    at = tile_at[firsts[p] + r] * (width // 8) + g
                    if m == 0:
                        added = jnp.where(low, a, pltpu.roll(c, HALF, 1))
                    else:
                        added = jnp.where(low, pltpu.roll(a, HALF, 1), c)
                    ens_v[m, at] = ens_v[m, at] + added
        store = pltpu.make_async_copy(ens_v.at[m], out_ref.at[m], sems.at[4 + m])
        store.start()
        stores.append(store)
    for store in stores:
        store.wait()


def filter_tiles(cfg, ens, obs_sites, owner, obs_values, obs_error):
    levels, count, parts, tiles, width, blocks, obs = cfg
    slots = sum(parts)
    n_obs = blocks * obs
    hbm = pl.BlockSpec(memory_space=pltpu.HBM)
    anywhere = pl.BlockSpec(memory_space=pl.ANY)
    dma = pltpu.SemaphoreType.DMA
    limit = VMEM_BYTES - 4 * count * slots * 128
    back = pl.pallas_call(
        functools.partial(exchange_kernel, cfg),
        out_shape=jax.ShapeDtypeStruct((count * slots, 128), F32),
        in_specs=[hbm] * 5,
        out_specs=anywhere,
        scratch_shapes=[
            pltpu.SMEM(obs_sites.shape, jnp.int32),
            pltpu.SMEM(owner.shape, jnp.int32),
            pltpu.SMEM(obs_values.shape, F32),
            pltpu.SMEM(obs_error.shape, F32),
            pltpu.VMEM(ens.shape, F32),
            pltpu.VMEM((count * slots, 128), F32),
            pltpu.VMEM((count * slots, 128), F32),
            pltpu.VMEM((count * slots, 128), F32),
            pltpu.VMEM((2 * n_obs, 128), F32),
            pltpu.VMEM((8 * levels, 128), F32),
            pltpu.VMEM((8, 128), F32),
            pltpu.VMEM((count, 128), F32),
            pltpu.VMEM((n_obs, n_obs, 128), F32),
            pltpu.VMEM((slots // 2, n_obs, 128), F32),
            pltpu.VMEM((n_obs, n_obs, 128), F32),
            pltpu.VMEM((slots // 2, n_obs, 128), F32),
            dma,
            dma((4,)),
            dma((levels,)),
            dma((levels,)),
            dma,
            dma,
            dma((len(parts),)),
            dma((len(parts),)),
            dma((len(parts),)),
            dma((len(parts),)),
            dma((len(parts),)),
        ],
        compiler_params=pltpu.CompilerParams(
            collective_id=slots, has_side_effects=True, vmem_limit_bytes=limit
        ),
    )(obs_sites, owner, obs_values, obs_error, ens)
    return pl.pallas_call(
        functools.partial(apply_kernel, cfg),
        out_shape=jax.ShapeDtypeStruct(ens.shape, F32),
        in_specs=[hbm, hbm, anywhere],
        out_specs=hbm,
        scratch_shapes=[
            pltpu.SMEM(owner.shape, jnp.int32),
            pltpu.VMEM(ens.shape, F32),
            pltpu.VMEM((count * slots, 128), F32),
            dma((6,)),
        ],
        compiler_params=pltpu.CompilerParams(vmem_limit_bytes=limit),
    )(owner, ens, back)


def shards(layouts, ensemble, obs_sites, owner, tile_mask, obs_values, obs_error):
    levels, count = lax.axis_size("lev"), lax.axis_size("var")
    _, m_dev, x_all, y_all = ensemble.shape
    blocks, obs = obs_sites.shape
    tiles = tile_mask.shape[1]
    ens = ensemble.reshape(m_dev, x_all // 8, 8, y_all)
    rest = (ens, obs_sites, owner, obs_values, obs_error)
    branches = [
        functools.partial(filter_tiles, (levels, count, parts, tiles, x_all // tiles, blocks, obs))
        for parts in layouts
    ]
    if len(layouts) == 1:
        out = branches[0](*rest)
    else:
        touched = jnp.sum(jnp.max(tile_mask, axis=0))
        which = sum((touched > sum(parts)).astype(jnp.int32) for parts in layouts[:-1])
        out = lax.switch(which, branches, *rest)
    return out.reshape(ensemble.shape)


def solution(mesh):
    in_specs = (P("lev", "var", None, None), P(), P(), P(), P(), P())
    out_specs = P("lev", "var", None, None)
    return jax.shard_map(
        functools.partial(shards, LAYOUTS),
        mesh=mesh,
        in_specs=in_specs,
        out_specs=out_specs,
        check_vma=False,
    )
```

```python
import functools

import jax
import jax.numpy as jnp
from jax import lax
from jax.experimental import pallas as pl
from jax.experimental.pallas import tpu as pltpu
from jax.sharding import PartitionSpec as P

MESH = pl.DeviceIdType.MESH
HIGHEST = lax.Precision.HIGHEST
F32 = jnp.float32
REACH = 3
PARTS = (8, 14)
MORE_PARTS = (6,)
VMEM_BYTES = 64 * 2**20
HALF = 64


def step_at(value, edge):
    return jnp.minimum(jnp.maximum(value - edge + 1, 0), 1)


def changed_tiles(owner_ref, blocks, tiles, start, slots):
    t = [owner_ref[b] & (tiles - 1) for b in range(blocks)]
    for i in range(blocks):
        for j in range(blocks - 1 - i):
            t[j], t[j + 1] = jnp.minimum(t[j], t[j + 1]), jnp.maximum(t[j], t[j + 1])
    befores, gaps, total, end = [], [], 0, -1
    for b in range(blocks):
        begin = jnp.maximum(jnp.maximum(t[b] - REACH, end + 1), 0)
        gaps.append(begin - end - 1)
        end = jnp.minimum(t[b] + REACH, tiles - 1)
        befores.append(total)
        total = total + jnp.maximum(end - begin + 1, 0)
    found = []
    for s in range(start, start + slots):
        tile = gaps[0] + s
        for b in range(1, blocks):
            tile = tile + gaps[b] * step_at(s, befores[b])
        found.append((tile + 1) * step_at(total - 1, s) - 1)
    return found, total


def places(parts, count):
    firsts = [sum(parts[:p]) for p in range(len(parts))]
    return firsts, [count * first for first in firsts]


def taper(dx, dy, radius):
    return jnp.square(jnp.maximum(0.0, 1.0 - (dx * dx + dy * dy) / (radius * radius)))


def exchange_kernel(
    cfg,
    sites_hbm,
    owner_hbm,
    values_hbm,
    errors_hbm,
    ens_ref,
    back_ref,
    more_hbm,
    sites_ref,
    owner_ref,
    values_ref,
    errors_ref,
    more_ref,
    ens_v,
    out_buf,
    in_buf,
    ret_buf,
    site_v,
    near_buf,
    row_buf,
    row_in,
    wcol_v,
    wcell_v,
    hcol_v,
    r_v,
    load_sem,
    small_sem,
    more_sem,
    near_send,
    near_recv,
    row_send,
    row_recv,
    bulk_send,
    bulk_recv,
    ret_send,
    ret_recv,
    own_sem,
):
    levels, count, start, parts, tiles, width, blocks, obs = cfg
    slots = sum(parts)
    n_obs = blocks * obs
    members = 2 * count
    lev = lax.axis_index("lev")
    me = lax.axis_index("var")
    radius = jnp.float32(REACH * width)
    tile_bits = tiles.bit_length() - 1
    firsts, bases = places(parts, count)

    load = pltpu.make_async_copy(ens_ref, ens_v, load_sem)
    small = [
        pltpu.make_async_copy(src, dst, small_sem.at[i])
        for i, (src, dst) in enumerate(
            [
                (owner_hbm, owner_ref),
                (sites_hbm, sites_ref),
                (values_hbm, values_ref),
                (errors_hbm, errors_ref),
            ]
        )
    ]
    for copy in small:
        copy.start()
    load.start()

    barrier = pltpu.get_barrier_semaphore()

    def greet(j, carry):
        pl.semaphore_signal(
            barrier, inc=1, device_id=(lev, lax.rem(me + j, count)), device_id_type=MESH
        )
        return carry

    lax.fori_loop(1, count, greet, 0)
    for j in range(1, levels):
        pl.semaphore_signal(
            barrier, inc=1, device_id=((lev + j) % levels, me), device_id_type=MESH
        )

    for copy in small:
        copy.wait()

    lane = lax.broadcasted_iota(jnp.int32, (1, 128), 1)
    low = lane < HALF
    tile_at, touched = changed_tiles(owner_ref, blocks, tiles, start, slots)
    more_ref[0] = step_at(touched - 1, start + slots)
    tell = pltpu.make_async_copy(more_ref, more_hbm, more_sem)
    tell.start()

    load.wait()

    for m in range(2):
        for i in range(n_obs):
            b, k = i // obs, i % obs
            site = sites_ref[b, k]
            away = (owner_ref[b] >> tile_bits) - lev
            row = ens_v[m, site >> 10, pl.ds((site >> 7) & 7, 1), :]
            site_v[pl.ds(m * n_obs + i, 1), :] = jnp.where(
                lane == (site & 127) + 128 * away, row, 0.0
            )
    sums = jnp.sum(site_v[...], axis=1, keepdims=True)
    sub64 = lax.broadcasted_iota(jnp.int32, (2 * n_obs, 128), 0)
    lane64 = lax.broadcasted_iota(jnp.int32, (2 * n_obs, 128), 1)
    mine = jnp.sum(jnp.where(sub64 == lane64, sums, 0.0), axis=0, keepdims=True)
    near_buf[pl.ds(0, 8), :] = jnp.broadcast_to(mine, (8, 128))

    for p, size in enumerate(parts):
        for r in range(size):
            tile = jnp.maximum(tile_at[firsts[p] + r], 0)
            for g in range(4):
                a = ens_v[0, tile * (width // 8) + g]
                c = ens_v[1, tile * (width // 8) + g]
                row = bases[p] + g * 16 * size + r
                out_buf[pl.ds(row, 8, stride=size), :] = jnp.where(low, a, pltpu.roll(c, HALF, 1))
                out_buf[pl.ds(row + 8 * size, 8, stride=size), :] = jnp.where(
                    low, pltpu.roll(a, HALF, 1), c
                )

    pl.semaphore_wait(barrier, count - 1 + levels - 1)

    near = []
    for j in range(1, levels):
        copy = pltpu.make_async_remote_copy(
            near_buf.at[pl.ds(0, 8)],
            near_buf.at[pl.ds(8 * j, 8)],
            near_send.at[j],
            near_recv.at[j],
            device_id=((lev + j) % levels, me),
            device_id_type=MESH,
        )
        copy.start()
        near.append(copy)

    def send_part(p, src, dst, send_sem, recv_sem):
        size = parts[p]

        def send(j, carry):
            to = lax.rem(me + j, count)
            pltpu.make_async_remote_copy(
                src.at[pl.ds(bases[p] + to * size, size)],
                dst.at[pl.ds(bases[p] + me * size, size)],
                send_sem.at[p],
                recv_sem.at[p],
                device_id=(lev, to),
                device_id_type=MESH,
            ).start()
            return carry

        lax.fori_loop(1, count, send, 0)

    def wait_part(p, buf, sem):
        rest = pl.ds(bases[p], (count - 1) * parts[p])
        pltpu.make_async_copy(buf.at[rest], buf.at[rest], sem.at[p]).wait()

    send_part(0, out_buf, in_buf, bulk_send, bulk_recv)
    for copy in near:
        copy.wait_recv()
    row_buf[...] = (near_buf[pl.ds(0, 8), :] + near_buf[pl.ds(8, 8), :]) + (
        near_buf[pl.ds(16, 8), :] + near_buf[pl.ds(24, 8), :]
    )

    def send_row(j, carry):
        to = lax.rem(me + j, count)
        pltpu.make_async_remote_copy(
            row_buf.at[pl.ds(0, 1)],
            row_in.at[pl.ds(me, 1)],
            row_send,
            row_recv,
            device_id=(lev, to),
            device_id_type=MESH,
        ).start()
        return carry

    lax.fori_loop(1, count, send_row, 0)
    for p in range(1, len(parts)):
        send_part(p, out_buf, in_buf, bulk_send, bulk_recv)
    row_in[pl.ds(me, 1), :] = row_buf[pl.ds(0, 1), :]
    for p, size in enumerate(parts):
        here = pl.ds(bases[p] + me * size, size)
        in_buf[here, :] = out_buf[here, :]
    sub32 = lax.broadcasted_iota(jnp.int32, (n_obs, 128), 0)
    lane32 = lax.broadcasted_iota(jnp.int32, (n_obs, 128), 1)
    site_c = jnp.zeros((n_obs, 128), jnp.int32)
    own_c = jnp.zeros((n_obs, 128), jnp.int32)
    err_c = jnp.zeros((n_obs, 128), F32)
    val_c = jnp.zeros((n_obs, 128), F32)
    site_r = jnp.zeros((1, 128), jnp.int32)
    own_r = jnp.zeros((1, 128), jnp.int32)
    for i in range(n_obs):
        b, k = i // obs, i % obs
        at = sub32 == i
        site_c = jnp.where(at, sites_ref[b, k], site_c)
        own_c = jnp.where(at, owner_ref[b], own_c)
        err_c = jnp.where(at, errors_ref[b, k], err_c)
        val_c = jnp.where(at, values_ref[b, k], val_c)
        site_r = jnp.where(lane == i, sites_ref[b, k], site_r)
        own_r = jnp.where(lane == i, owner_ref[b], own_r)
    x_c = (site_c >> 7).astype(F32)
    y_c = (site_c & 127).astype(F32)
    t_c = own_c & (tiles - 1)
    l_c = own_c >> tile_bits
    x_r = (site_r >> 7).astype(F32)
    y_r = (site_r & 127).astype(F32)
    t_r = own_r & (tiles - 1)
    l_r = own_r >> tile_bits
    pair_w = (
        jnp.where(jnp.abs(t_c - t_r) <= REACH, 1.0, 0.0)
        * jnp.exp2(-jnp.abs(l_c - l_r).astype(F32))
        * taper(x_c - x_r, y_c - y_r, radius)
    )
    row_w = jnp.where((lane32 > sub32) & (lane32 < n_obs), pair_w, 0.0)
    for k in range(n_obs):
        b = k // obs
        site = sites_ref[b, k % obs]
        own = owner_ref[b]
        w = (
            jnp.where(jnp.abs(t_c - (own & (tiles - 1))) <= REACH, 1.0, 0.0)
            * jnp.exp2(-jnp.abs(l_c - (own >> tile_bits)).astype(F32))
            * taper(x_c - (site >> 7).astype(F32), y_c - (site & 127).astype(F32), radius)
        )
        wcol_v[k] = jnp.where(sub32 > k, w, 0.0)

    group, side, column = me // 16, (me // 8) % 2, me % 8
    cell_y = (side * HALF + lane % HALF).astype(F32)
    level_f = jnp.exp2(-jnp.abs(l_c - lev).astype(F32))
    for p in range(slots // 2):
        tile = jnp.where(low, tile_at[2 * p], tile_at[2 * p + 1])
        cell_x = (tile * width + group * 8 + column).astype(F32)
        inside = (tile >= 0) & (jnp.abs(t_c - tile) <= REACH)
        wcell_v[p] = (
            jnp.where(inside, 1.0, 0.0) * level_f * taper(cell_x - x_c, cell_y - y_c, radius)
        )

    for copy in near:
        copy.wait_send()
    pltpu.make_async_copy(
        row_in.at[pl.ds(0, count - 1)], row_in.at[pl.ds(0, count - 1)], row_recv
    ).wait()

    raw = row_in[...]
    total = jnp.sum(raw, axis=0, keepdims=True)
    both = jnp.where(lane < n_obs, total + pltpu.roll(total, 128 - n_obs, 1), 0.0)
    mean_r = both / members
    mean2_r = mean_r + pltpu.roll(mean_r, n_obs, 1)
    centred = jnp.where(lane < 2 * n_obs, raw - mean2_r, 0.0)
    full = lax.dot_general(
        centred, centred, (((0,), (0,)), ((), ())), precision=HIGHEST, preferred_element_type=F32
    )
    gram = full[:n_obs] + pltpu.roll(full[n_obs : 2 * n_obs], 128 - n_obs, 1)
    gram = jnp.where(lane < n_obs, gram, 0.0)
    mean_c = jnp.sum(jnp.where(sub32 == lane32, mean_r, 0.0), axis=1, keepdims=True)
    mean_c = jnp.broadcast_to(mean_c, (n_obs, 128))
    mix = jnp.where(sub32 == lane32, 1.0, 0.0)
    alpha_c = jnp.zeros((n_obs, 128), F32)
    beta_c = jnp.zeros((n_obs, 128), F32)
    inv_c = jnp.zeros((n_obs, 128), F32)
    beta_r = jnp.zeros((1, 128), F32)
    for k in range(n_obs):
        u_row = gram[k : k + 1, :]
        u_col = jnp.broadcast_to(gram[:, k : k + 1], (n_obs, 128))
        d = u_col[k : k + 1, :]
        spread = d / (members - 1) + 1e-06
        r = err_c[k : k + 1, :]
        inv = 1.0 / (spread + r)
        alpha = spread * inv * (val_c[k : k + 1, :] - mean_c[k : k + 1, :])
        beta = jnp.sqrt(r * inv) - 1.0
        inv_scaled = 1.0 / ((members - 1) * spread)
        c_col = wcol_v[k] * u_col * inv_scaled
        g_row = row_w[k : k + 1, :] * u_row * (inv_scaled * beta)
        g_col = c_col * beta
        mean_c = mean_c + c_col * alpha
        gram = gram + (g_col * (u_row + g_row * d) + u_col * g_row)
        mix = mix + g_col * mix[k : k + 1, :]
        at = sub32 == k
        alpha_c = jnp.where(at, alpha, alpha_c)
        beta_c = jnp.where(at, beta, beta_c)
        inv_c = jnp.where(at, inv_scaled, inv_c)
        beta_r = jnp.where(lane == k, beta, beta_r)
    lower = jnp.where(lane32 < sub32, gram * beta_r, 0.0)
    for k in range(n_obs):
        hcol_v[k] = jnp.broadcast_to(lower[:, k : k + 1], (n_obs, 128))

    mix2 = jnp.concatenate([mix, pltpu.roll(mix, n_obs, 1)], axis=0)
    anomalies = lax.dot_general(
        mix2, centred, (((1,), (1,)), ((), ())), precision=HIGHEST, preferred_element_type=F32
    )
    shift = (
        jnp.concatenate([alpha_c, alpha_c], axis=0)[:, :count]
        + jnp.concatenate([beta_c, beta_c], axis=0)[:, :count] * anomalies
    )

    def half_sum(part):
        t = jnp.where(low, part[:n_obs], part[n_obs:])
        return t + pltpu.roll(t, HALF, 1)

    own = []
    for p, size in enumerate(parts):
        wait_part(p, in_buf, bulk_recv)
        for q in range(size // 2):
            row = bases[p] + 2 * q
            x = jnp.concatenate(
                [
                    in_buf[pl.ds(row, count, stride=size), :],
                    in_buf[pl.ds(row + 1, count, stride=size), :],
                ],
                axis=1,
            )
            r2 = jnp.dot(anomalies, x, precision=HIGHEST, preferred_element_type=F32)
            r_v[firsts[p] // 2 + q] = jnp.where(low, half_sum(r2[:, :128]), half_sum(r2[:, 128:]))

        for q in range(size // 2):
            row = bases[p] + 2 * q
            reg = r_v[firsts[p] // 2 + q]
            w = wcell_v[firsts[p] // 2 + q] * inv_c
            for k in range(n_obs - 1):
                reg = reg + hcol_v[k] * (w[k : k + 1, :] * reg[k : k + 1, :])
            coefs = w * reg
            turned = pltpu.roll(coefs, HALF, 1)
            zero = jnp.zeros_like(coefs)
            first = jnp.concatenate(
                [jnp.where(low, coefs, zero), jnp.where(low, zero, turned)], axis=0
            )
            second = jnp.concatenate(
                [jnp.where(low, turned, zero), jnp.where(low, zero, coefs)], axis=0
            )
            delta = lax.dot_general(
                shift,
                jnp.concatenate([first, second], axis=1),
                (((0,), (0,)), ((), ())),
                precision=HIGHEST,
                preferred_element_type=F32,
            )
            ret_buf[pl.ds(row, count, stride=size), :] = delta[:, :128]
            ret_buf[pl.ds(row + 1, count, stride=size), :] = delta[:, 128:]

        send_part(p, ret_buf, back_ref, ret_send, ret_recv)
        here = pl.ds(bases[p] + me * size, size)
        copy = pltpu.make_async_copy(ret_buf.at[here], back_ref.at[here], own_sem.at[p])
        copy.start()
        own.append(copy)

    tell.wait()
    rows = row_in.at[pl.ds(0, count - 1)]
    pltpu.make_async_copy(rows, rows, row_send).wait()
    for p in range(len(parts)):
        wait_part(p, out_buf, bulk_send)
        own[p].wait()
    for p in range(len(parts)):
        wait_part(p, back_ref, ret_recv)
    for p in range(len(parts)):
        wait_part(p, ret_buf, ret_send)


def apply_kernel(cfgs, owner_hbm, ens_ref, *refs):
    n = len(cfgs)
    backs, out_ref, owner_ref, ens_v, kept, sems = (
        refs[:n],
        refs[n],
        refs[n + 1],
        refs[n + 2],
        refs[n + 3 : 2 * n + 3],
        refs[2 * n + 3],
    )
    small = pltpu.make_async_copy(owner_hbm, owner_ref, sems.at[0])
    small.start()
    load_backs = [
        pltpu.make_async_copy(backs[i], kept[i], sems.at[5 + i]) for i in range(n)
    ]
    loads = [
        pltpu.make_async_copy(ens_ref.at[m], ens_v.at[m], sems.at[1 + m]) for m in range(2)
    ]
    for load in load_backs + loads:
        load.start()
    small.wait()
    low = lax.broadcasted_iota(jnp.int32, (1, 128), 1) < HALF
    for load in load_backs:
        load.wait()
    stores = []
    for m in range(2):
        loads[m].wait()
        for i, (levels, count, start, parts, tiles, width, blocks, obs) in enumerate(cfgs):
            firsts, bases = places(parts, count)
            tile_at, _ = changed_tiles(owner_ref, blocks, tiles, start, sum(parts))
            for p, size in enumerate(parts):
                for r in range(size):
                    tile = jnp.maximum(tile_at[firsts[p] + r], 0)
                    for g in range(4):
                        row = bases[p] + g * 16 * size + r
                        a = kept[i][pl.ds(row, 8, stride=size), :]
                        c = kept[i][pl.ds(row + 8 * size, 8, stride=size), :]
                        at = tile * (width // 8) + g
                        if m == 0:
                            added = jnp.where(low, a, pltpu.roll(c, HALF, 1))
                        else:
                            added = jnp.where(low, pltpu.roll(a, HALF, 1), c)
                        ens_v[m, at] = ens_v[m, at] + added
        store = pltpu.make_async_copy(ens_v.at[m], out_ref.at[m], sems.at[3 + m])
        store.start()
        stores.append(store)
    for store in stores:
        store.wait()


def exchange(cfg, ens, obs_sites, owner, obs_values, obs_error):
    levels, count, start, parts, tiles, width, blocks, obs = cfg
    slots = sum(parts)
    n_obs = blocks * obs
    hbm = pl.BlockSpec(memory_space=pltpu.HBM)
    anywhere = pl.BlockSpec(memory_space=pl.ANY)
    dma = pltpu.SemaphoreType.DMA
    limit = VMEM_BYTES - 4 * count * slots * 128
    return pl.pallas_call(
        functools.partial(exchange_kernel, cfg),
        out_shape=(
            jax.ShapeDtypeStruct((count * slots, 128), F32),
            jax.ShapeDtypeStruct((1,), jnp.int32),
        ),
        in_specs=[hbm] * 5,
        out_specs=(anywhere, hbm),
        scratch_shapes=[
            pltpu.SMEM(obs_sites.shape, jnp.int32),
            pltpu.SMEM(owner.shape, jnp.int32),
            pltpu.SMEM(obs_values.shape, F32),
            pltpu.SMEM(obs_error.shape, F32),
            pltpu.SMEM((1,), jnp.int32),
            pltpu.VMEM(ens.shape, F32),
            pltpu.VMEM((count * slots, 128), F32),
            pltpu.VMEM((count * slots, 128), F32),
            pltpu.VMEM((count * slots, 128), F32),
            pltpu.VMEM((2 * n_obs, 128), F32),
            pltpu.VMEM((8 * levels, 128), F32),
            pltpu.VMEM((8, 128), F32),
            pltpu.VMEM((count, 128), F32),
            pltpu.VMEM((n_obs, n_obs, 128), F32),
            pltpu.VMEM((slots // 2, n_obs, 128), F32),
            pltpu.VMEM((n_obs, n_obs, 128), F32),
            pltpu.VMEM((slots // 2, n_obs, 128), F32),
            dma,
            dma((4,)),
            dma,
            dma((levels,)),
            dma((levels,)),
            dma,
            dma,
            dma((len(parts),)),
            dma((len(parts),)),
            dma((len(parts),)),
            dma((len(parts),)),
            dma((len(parts),)),
        ],
        compiler_params=pltpu.CompilerParams(
            collective_id=1 + start, has_side_effects=True, vmem_limit_bytes=limit
        ),
    )(obs_sites, owner, obs_values, obs_error, ens)


def apply(cfgs, owner, ens, *backs):
    hbm = pl.BlockSpec(memory_space=pltpu.HBM)
    anywhere = pl.BlockSpec(memory_space=pl.ANY)
    dma = pltpu.SemaphoreType.DMA
    return pl.pallas_call(
        functools.partial(apply_kernel, cfgs),
        out_shape=jax.ShapeDtypeStruct(ens.shape, F32),
        in_specs=[hbm, hbm] + [anywhere] * len(backs),
        out_specs=hbm,
        scratch_shapes=[
            pltpu.SMEM(owner.shape, jnp.int32),
            pltpu.VMEM(ens.shape, F32),
            *[pltpu.VMEM(back.shape, F32) for back in backs],
            dma((5 + len(backs),)),
        ],
        compiler_params=pltpu.CompilerParams(
            vmem_limit_bytes=VMEM_BYTES - 4 * sum(back.size for back in backs)
        ),
    )(owner, ens, *backs)


def shards(ensemble, obs_sites, owner, tile_mask, obs_values, obs_error):
    levels, count = lax.axis_size("lev"), lax.axis_size("var")
    _, m_dev, x_all, y_all = ensemble.shape
    blocks, obs = obs_sites.shape
    tiles = tile_mask.shape[1]
    ens = ensemble.reshape(m_dev, x_all // 8, 8, y_all)
    here = (tiles, x_all // tiles, blocks, obs)
    cfg = (levels, count, 0, PARTS, *here)
    more_cfg = (levels, count, sum(PARTS), MORE_PARTS, *here)
    back, more = exchange(cfg, ens, obs_sites, owner, obs_values, obs_error)

    def with_more():
        more_back, _ = exchange(more_cfg, ens, obs_sites, owner, obs_values, obs_error)
        return apply((cfg, more_cfg), owner, ens, back, more_back)

    out = lax.cond(more[0] > 0, with_more, lambda: apply((cfg,), owner, ens, back))
    return out.reshape(ensemble.shape)


def solution(mesh):
    in_specs = (P("lev", "var", None, None), P(), P(), P(), P(), P())
    out_specs = P("lev", "var", None, None)
    return jax.shard_map(
        shards,
        mesh=mesh,
        in_specs=in_specs,
        out_specs=out_specs,
        check_vma=False,
    )
```

```python
import functools

import jax
import jax.numpy as jnp
from jax import lax
from jax.experimental import pallas as pl
from jax.experimental.pallas import tpu as pltpu
from jax.sharding import PartitionSpec as P

MESH = pl.DeviceIdType.MESH
HIGHEST = lax.Precision.HIGHEST
F32 = jnp.float32
REACH = 3
PARTS = (8, 14)
MORE_PARTS = (6,)
VMEM_BYTES = 64 * 2**20
HALF = 64


def step_at(value, edge):
    return jnp.minimum(jnp.maximum(value - edge + 1, 0), 1)


def changed_tiles(owner_ref, blocks, tiles, start, slots):
    t = [owner_ref[b] & (tiles - 1) for b in range(blocks)]
    for i in range(blocks):
        for j in range(blocks - 1 - i):
            t[j], t[j + 1] = jnp.minimum(t[j], t[j + 1]), jnp.maximum(t[j], t[j + 1])
    befores, gaps, total, end = [], [], 0, -1
    for b in range(blocks):
        begin = jnp.maximum(jnp.maximum(t[b] - REACH, end + 1), 0)
        gaps.append(begin - end - 1)
        end = jnp.minimum(t[b] + REACH, tiles - 1)
        befores.append(total)
        total = total + jnp.maximum(end - begin + 1, 0)
    found = []
    for s in range(start, start + slots):
        tile = gaps[0] + s
        for b in range(1, blocks):
            tile = tile + gaps[b] * step_at(s, befores[b])
        found.append((tile + 1) * step_at(total - 1, s) - 1)
    return found, total


def places(parts, count):
    firsts = [sum(parts[:p]) for p in range(len(parts))]
    return firsts, [count * first for first in firsts]


def taper(dx, dy, radius):
    return jnp.square(jnp.maximum(0.0, 1.0 - (dx * dx + dy * dy) / (radius * radius)))


def exchange_kernel(
    cfg,
    sites_hbm,
    owner_hbm,
    values_hbm,
    errors_hbm,
    ens_ref,
    back_ref,
    more_hbm,
    sites_ref,
    owner_ref,
    values_ref,
    errors_ref,
    more_ref,
    ens_v,
    out_buf,
    in_buf,
    ret_buf,
    site_v,
    near_buf,
    row_buf,
    row_in,
    wcol_v,
    wcell_v,
    hcol_v,
    r_v,
    load_sem,
    small_sem,
    more_sem,
    near_send,
    near_recv,
    row_send,
    row_recv,
    bulk_send,
    bulk_recv,
    ret_send,
    ret_recv,
    own_sem,
):
    levels, count, start, parts, tiles, width, blocks, obs = cfg
    slots = sum(parts)
    n_obs = blocks * obs
    members = 2 * count
    lev = lax.axis_index("lev")
    me = lax.axis_index("var")
    radius = jnp.float32(REACH * width)
    tile_bits = tiles.bit_length() - 1
    firsts, bases = places(parts, count)

    load = pltpu.make_async_copy(ens_ref, ens_v, load_sem)
    small = [
        pltpu.make_async_copy(src, dst, small_sem.at[i])
        for i, (src, dst) in enumerate(
            [
                (owner_hbm, owner_ref),
                (sites_hbm, sites_ref),
                (values_hbm, values_ref),
                (errors_hbm, errors_ref),
            ]
        )
    ]
    for copy in small:
        copy.start()
    load.start()

    barrier = pltpu.get_barrier_semaphore()

    def greet(j, carry):
        pl.semaphore_signal(
            barrier, inc=1, device_id=(lev, lax.rem(me + j, count)), device_id_type=MESH
        )
        return carry

    lax.fori_loop(1, count, greet, 0)
    for j in range(1, levels):
        pl.semaphore_signal(
            barrier, inc=1, device_id=((lev + j) % levels, me), device_id_type=MESH
        )

    for copy in small:
        copy.wait()

    lane = lax.broadcasted_iota(jnp.int32, (1, 128), 1)
    low = lane < HALF
    tile_at, touched = changed_tiles(owner_ref, blocks, tiles, start, slots)
    more_ref[0] = step_at(touched - 1, start + slots)
    tell = pltpu.make_async_copy(more_ref, more_hbm, more_sem)
    tell.start()

    load.wait()

    for m in range(2):
        for i in range(n_obs):
            b, k = i // obs, i % obs
            site = sites_ref[b, k]
            away = (owner_ref[b] >> tile_bits) - lev
            row = ens_v[m, site >> 10, pl.ds((site >> 7) & 7, 1), :]
            site_v[pl.ds(m * n_obs + i, 1), :] = jnp.where(
                lane == (site & 127) + 128 * away, row, 0.0
            )
    sums = jnp.sum(site_v[...], axis=1, keepdims=True)
    sub64 = lax.broadcasted_iota(jnp.int32, (2 * n_obs, 128), 0)
    lane64 = lax.broadcasted_iota(jnp.int32, (2 * n_obs, 128), 1)
    mine = jnp.sum(jnp.where(sub64 == lane64, sums, 0.0), axis=0, keepdims=True)
    near_buf[pl.ds(0, 8), :] = jnp.broadcast_to(mine, (8, 128))

    def lay_out(p):
        size = parts[p]
        for r in range(size):
            tile = jnp.maximum(tile_at[firsts[p] + r], 0)
            for g in range(4):
                a = ens_v[0, tile * (width // 8) + g]
                c = ens_v[1, tile * (width // 8) + g]
                row = bases[p] + g * 16 * size + r
                out_buf[pl.ds(row, 8, stride=size), :] = jnp.where(low, a, pltpu.roll(c, HALF, 1))
                out_buf[pl.ds(row + 8 * size, 8, stride=size), :] = jnp.where(
                    low, pltpu.roll(a, HALF, 1), c
                )

    pl.semaphore_wait(barrier, count - 1 + levels - 1)

    near = []
    for j in range(1, levels):
        copy = pltpu.make_async_remote_copy(
            near_buf.at[pl.ds(0, 8)],
            near_buf.at[pl.ds(8 * j, 8)],
            near_send.at[j],
            near_recv.at[j],
            device_id=((lev + j) % levels, me),
            device_id_type=MESH,
        )
        copy.start()
        near.append(copy)

    def send_part(p, src, dst, send_sem, recv_sem):
        size = parts[p]

        def send(j, carry):
            to = lax.rem(me + j, count)
            pltpu.make_async_remote_copy(
                src.at[pl.ds(bases[p] + to * size, size)],
                dst.at[pl.ds(bases[p] + me * size, size)],
                send_sem.at[p],
                recv_sem.at[p],
                device_id=(lev, to),
                device_id_type=MESH,
            ).start()
            return carry

        lax.fori_loop(1, count, send, 0)

    def wait_part(p, buf, sem):
        rest = pl.ds(bases[p], (count - 1) * parts[p])
        pltpu.make_async_copy(buf.at[rest], buf.at[rest], sem.at[p]).wait()

    lay_out(0)
    send_part(0, out_buf, in_buf, bulk_send, bulk_recv)
    for p in range(1, len(parts)):
        lay_out(p)
    for copy in near:
        copy.wait_recv()
    row_buf[...] = (near_buf[pl.ds(0, 8), :] + near_buf[pl.ds(8, 8), :]) + (
        near_buf[pl.ds(16, 8), :] + near_buf[pl.ds(24, 8), :]
    )

    def send_row(j, carry):
        to = lax.rem(me + j, count)
        pltpu.make_async_remote_copy(
            row_buf.at[pl.ds(0, 1)],
            row_in.at[pl.ds(me, 1)],
            row_send,
            row_recv,
            device_id=(lev, to),
            device_id_type=MESH,
        ).start()
        return carry

    lax.fori_loop(1, count, send_row, 0)
    for p in range(1, len(parts)):
        send_part(p, out_buf, in_buf, bulk_send, bulk_recv)
    row_in[pl.ds(me, 1), :] = row_buf[pl.ds(0, 1), :]
    for p, size in enumerate(parts):
        here = pl.ds(bases[p] + me * size, size)
        in_buf[here, :] = out_buf[here, :]
    sub32 = lax.broadcasted_iota(jnp.int32, (n_obs, 128), 0)
    lane32 = lax.broadcasted_iota(jnp.int32, (n_obs, 128), 1)
    site_c = jnp.zeros((n_obs, 128), jnp.int32)
    own_c = jnp.zeros((n_obs, 128), jnp.int32)
    err_c = jnp.zeros((n_obs, 128), F32)
    val_c = jnp.zeros((n_obs, 128), F32)
    site_r = jnp.zeros((1, 128), jnp.int32)
    own_r = jnp.zeros((1, 128), jnp.int32)
    for i in range(n_obs):
        b, k = i // obs, i % obs
        at = sub32 == i
        site_c = jnp.where(at, sites_ref[b, k], site_c)
        own_c = jnp.where(at, owner_ref[b], own_c)
        err_c = jnp.where(at, errors_ref[b, k], err_c)
        val_c = jnp.where(at, values_ref[b, k], val_c)
        site_r = jnp.where(lane == i, sites_ref[b, k], site_r)
        own_r = jnp.where(lane == i, owner_ref[b], own_r)
    x_c = (site_c >> 7).astype(F32)
    y_c = (site_c & 127).astype(F32)
    t_c = own_c & (tiles - 1)
    l_c = own_c >> tile_bits
    x_r = (site_r >> 7).astype(F32)
    y_r = (site_r & 127).astype(F32)
    t_r = own_r & (tiles - 1)
    l_r = own_r >> tile_bits
    pair_w = (
        jnp.where(jnp.abs(t_c - t_r) <= REACH, 1.0, 0.0)
        * jnp.exp2(-jnp.abs(l_c - l_r).astype(F32))
        * taper(x_c - x_r, y_c - y_r, radius)
    )
    row_w = jnp.where((lane32 > sub32) & (lane32 < n_obs), pair_w, 0.0)
    for k in range(n_obs):
        b = k // obs
        site = sites_ref[b, k % obs]
        own = owner_ref[b]
        w = (
            jnp.where(jnp.abs(t_c - (own & (tiles - 1))) <= REACH, 1.0, 0.0)
            * jnp.exp2(-jnp.abs(l_c - (own >> tile_bits)).astype(F32))
            * taper(x_c - (site >> 7).astype(F32), y_c - (site & 127).astype(F32), radius)
        )
        wcol_v[k] = jnp.where(sub32 > k, w, 0.0)

    group, side, column = me // 16, (me // 8) % 2, me % 8
    cell_y = (side * HALF + lane % HALF).astype(F32)
    level_f = jnp.exp2(-jnp.abs(l_c - lev).astype(F32))
    for p in range(slots // 2):
        tile = jnp.where(low, tile_at[2 * p], tile_at[2 * p + 1])
        cell_x = (tile * width + group * 8 + column).astype(F32)
        inside = (tile >= 0) & (jnp.abs(t_c - tile) <= REACH)
        wcell_v[p] = (
            jnp.where(inside, 1.0, 0.0) * level_f * taper(cell_x - x_c, cell_y - y_c, radius)
        )

    for copy in near:
        copy.wait_send()
    pltpu.make_async_copy(
        row_in.at[pl.ds(0, count - 1)], row_in.at[pl.ds(0, count - 1)], row_recv
    ).wait()

    raw = row_in[...]
    total = jnp.sum(raw, axis=0, keepdims=True)
    both = jnp.where(lane < n_obs, total + pltpu.roll(total, 128 - n_obs, 1), 0.0)
    mean_r = both / members
    mean2_r = mean_r + pltpu.roll(mean_r, n_obs, 1)
    centred = jnp.where(lane < 2 * n_obs, raw - mean2_r, 0.0)
    full = lax.dot_general(
        centred, centred, (((0,), (0,)), ((), ())), precision=HIGHEST, preferred_element_type=F32
    )
    gram = full[:n_obs] + pltpu.roll(full[n_obs : 2 * n_obs], 128 - n_obs, 1)
    gram = jnp.where(lane < n_obs, gram, 0.0)
    mean_c = jnp.sum(jnp.where(sub32 == lane32, mean_r, 0.0), axis=1, keepdims=True)
    mean_c = jnp.broadcast_to(mean_c, (n_obs, 128))
    mix = jnp.where(sub32 == lane32, 1.0, 0.0)
    alpha_c = jnp.zeros((n_obs, 128), F32)
    beta_c = jnp.zeros((n_obs, 128), F32)
    inv_c = jnp.zeros((n_obs, 128), F32)
    beta_r = jnp.zeros((1, 128), F32)
    for k in range(n_obs):
        u_row = gram[k : k + 1, :]
        u_col = jnp.broadcast_to(gram[:, k : k + 1], (n_obs, 128))
        d = u_col[k : k + 1, :]
        spread = d / (members - 1) + 1e-06
        r = err_c[k : k + 1, :]
        inv = 1.0 / (spread + r)
        alpha = spread * inv * (val_c[k : k + 1, :] - mean_c[k : k + 1, :])
        beta = jnp.sqrt(r * inv) - 1.0
        inv_scaled = 1.0 / ((members - 1) * spread)
        c_col = wcol_v[k] * u_col * inv_scaled
        g_row = row_w[k : k + 1, :] * u_row * (inv_scaled * beta)
        g_col = c_col * beta
        mean_c = mean_c + c_col * alpha
        gram = gram + (g_col * (u_row + g_row * d) + u_col * g_row)
        mix = mix + g_col * mix[k : k + 1, :]
        at = sub32 == k
        alpha_c = jnp.where(at, alpha, alpha_c)
        beta_c = jnp.where(at, beta, beta_c)
        inv_c = jnp.where(at, inv_scaled, inv_c)
        beta_r = jnp.where(lane == k, beta, beta_r)
    lower = jnp.where(lane32 < sub32, gram * beta_r, 0.0)
    for k in range(n_obs):
        hcol_v[k] = jnp.broadcast_to(lower[:, k : k + 1], (n_obs, 128))

    mix2 = jnp.concatenate([mix, pltpu.roll(mix, n_obs, 1)], axis=0)
    anomalies = lax.dot_general(
        mix2, centred, (((1,), (1,)), ((), ())), precision=HIGHEST, preferred_element_type=F32
    )
    shift = (
        jnp.concatenate([alpha_c, alpha_c], axis=0)[:, :count]
        + jnp.concatenate([beta_c, beta_c], axis=0)[:, :count] * anomalies
    )

    def half_sum(part):
        t = jnp.where(low, part[:n_obs], part[n_obs:])
        return t + pltpu.roll(t, HALF, 1)

    own = []
    for p, size in enumerate(parts):
        wait_part(p, in_buf, bulk_recv)
        for q in range(size // 2):
            row = bases[p] + 2 * q
            x = jnp.concatenate(
                [
                    in_buf[pl.ds(row, count, stride=size), :],
                    in_buf[pl.ds(row + 1, count, stride=size), :],
                ],
                axis=1,
            )
            r2 = jnp.dot(anomalies, x, precision=HIGHEST, preferred_element_type=F32)
            r_v[firsts[p] // 2 + q] = jnp.where(low, half_sum(r2[:, :128]), half_sum(r2[:, 128:]))

        for q in range(size // 2):
            row = bases[p] + 2 * q
            reg = r_v[firsts[p] // 2 + q]
            w = wcell_v[firsts[p] // 2 + q] * inv_c
            for k in range(n_obs - 1):
                reg = reg + hcol_v[k] * (w[k : k + 1, :] * reg[k : k + 1, :])
            coefs = w * reg
            turned = pltpu.roll(coefs, HALF, 1)
            zero = jnp.zeros_like(coefs)
            first = jnp.concatenate(
                [jnp.where(low, coefs, zero), jnp.where(low, zero, turned)], axis=0
            )
            second = jnp.concatenate(
                [jnp.where(low, turned, zero), jnp.where(low, zero, coefs)], axis=0
            )
            delta = lax.dot_general(
                shift,
                jnp.concatenate([first, second], axis=1),
                (((0,), (0,)), ((), ())),
                precision=HIGHEST,
                preferred_element_type=F32,
            )
            ret_buf[pl.ds(row, count, stride=size), :] = delta[:, :128]
            ret_buf[pl.ds(row + 1, count, stride=size), :] = delta[:, 128:]

        send_part(p, ret_buf, back_ref, ret_send, ret_recv)
        here = pl.ds(bases[p] + me * size, size)
        copy = pltpu.make_async_copy(ret_buf.at[here], back_ref.at[here], own_sem.at[p])
        copy.start()
        own.append(copy)

    tell.wait()
    rows = row_in.at[pl.ds(0, count - 1)]
    pltpu.make_async_copy(rows, rows, row_send).wait()
    for p in range(len(parts)):
        wait_part(p, out_buf, bulk_send)
        own[p].wait()
    for p in range(len(parts)):
        wait_part(p, back_ref, ret_recv)
    for p in range(len(parts)):
        wait_part(p, ret_buf, ret_send)


def apply_kernel(cfgs, owner_hbm, ens_ref, *refs):
    n = len(cfgs)
    backs, out_ref, owner_ref, ens_v, kept, sems = (
        refs[:n],
        refs[n],
        refs[n + 1],
        refs[n + 2],
        refs[n + 3 : 2 * n + 3],
        refs[2 * n + 3],
    )
    small = pltpu.make_async_copy(owner_hbm, owner_ref, sems.at[0])
    small.start()
    load_backs = [
        pltpu.make_async_copy(backs[i], kept[i], sems.at[5 + i]) for i in range(n)
    ]
    loads = [
        pltpu.make_async_copy(ens_ref.at[m], ens_v.at[m], sems.at[1 + m]) for m in range(2)
    ]
    for load in load_backs + loads:
        load.start()
    small.wait()
    low = lax.broadcasted_iota(jnp.int32, (1, 128), 1) < HALF
    for load in load_backs:
        load.wait()
    stores = []
    for m in range(2):
        loads[m].wait()
        for i, (levels, count, start, parts, tiles, width, blocks, obs) in enumerate(cfgs):
            firsts, bases = places(parts, count)
            tile_at, _ = changed_tiles(owner_ref, blocks, tiles, start, sum(parts))
            for p, size in enumerate(parts):
                for r in range(size):
                    tile = jnp.maximum(tile_at[firsts[p] + r], 0)
                    for g in range(4):
                        row = bases[p] + g * 16 * size + r
                        a = kept[i][pl.ds(row, 8, stride=size), :]
                        c = kept[i][pl.ds(row + 8 * size, 8, stride=size), :]
                        at = tile * (width // 8) + g
                        if m == 0:
                            added = jnp.where(low, a, pltpu.roll(c, HALF, 1))
                        else:
                            added = jnp.where(low, pltpu.roll(a, HALF, 1), c)
                        ens_v[m, at] = ens_v[m, at] + added
        store = pltpu.make_async_copy(ens_v.at[m], out_ref.at[m], sems.at[3 + m])
        store.start()
        stores.append(store)
    for store in stores:
        store.wait()


def exchange(cfg, ens, obs_sites, owner, obs_values, obs_error):
    levels, count, start, parts, tiles, width, blocks, obs = cfg
    slots = sum(parts)
    n_obs = blocks * obs
    hbm = pl.BlockSpec(memory_space=pltpu.HBM)
    anywhere = pl.BlockSpec(memory_space=pl.ANY)
    dma = pltpu.SemaphoreType.DMA
    limit = VMEM_BYTES - 4 * count * slots * 128
    return pl.pallas_call(
        functools.partial(exchange_kernel, cfg),
        out_shape=(
            jax.ShapeDtypeStruct((count * slots, 128), F32),
            jax.ShapeDtypeStruct((1,), jnp.int32),
        ),
        in_specs=[hbm] * 5,
        out_specs=(anywhere, hbm),
        scratch_shapes=[
            pltpu.SMEM(obs_sites.shape, jnp.int32),
            pltpu.SMEM(owner.shape, jnp.int32),
            pltpu.SMEM(obs_values.shape, F32),
            pltpu.SMEM(obs_error.shape, F32),
            pltpu.SMEM((1,), jnp.int32),
            pltpu.VMEM(ens.shape, F32),
            pltpu.VMEM((count * slots, 128), F32),
            pltpu.VMEM((count * slots, 128), F32),
            pltpu.VMEM((count * slots, 128), F32),
            pltpu.VMEM((2 * n_obs, 128), F32),
            pltpu.VMEM((8 * levels, 128), F32),
            pltpu.VMEM((8, 128), F32),
            pltpu.VMEM((count, 128), F32),
            pltpu.VMEM((n_obs, n_obs, 128), F32),
            pltpu.VMEM((slots // 2, n_obs, 128), F32),
            pltpu.VMEM((n_obs, n_obs, 128), F32),
            pltpu.VMEM((slots // 2, n_obs, 128), F32),
            dma,
            dma((4,)),
            dma,
            dma((levels,)),
            dma((levels,)),
            dma,
            dma,
            dma((len(parts),)),
            dma((len(parts),)),
            dma((len(parts),)),
            dma((len(parts),)),
            dma((len(parts),)),
        ],
        compiler_params=pltpu.CompilerParams(
            collective_id=1 + start, has_side_effects=True, vmem_limit_bytes=limit
        ),
    )(obs_sites, owner, obs_values, obs_error, ens)


def apply(cfgs, owner, ens, *backs):
    hbm = pl.BlockSpec(memory_space=pltpu.HBM)
    anywhere = pl.BlockSpec(memory_space=pl.ANY)
    dma = pltpu.SemaphoreType.DMA
    return pl.pallas_call(
        functools.partial(apply_kernel, cfgs),
        out_shape=jax.ShapeDtypeStruct(ens.shape, F32),
        in_specs=[hbm, hbm] + [anywhere] * len(backs),
        out_specs=hbm,
        scratch_shapes=[
            pltpu.SMEM(owner.shape, jnp.int32),
            pltpu.VMEM(ens.shape, F32),
            *[pltpu.VMEM(back.shape, F32) for back in backs],
            dma((5 + len(backs),)),
        ],
        compiler_params=pltpu.CompilerParams(
            vmem_limit_bytes=VMEM_BYTES - 4 * sum(back.size for back in backs)
        ),
    )(owner, ens, *backs)


def shards(ensemble, obs_sites, owner, tile_mask, obs_values, obs_error):
    levels, count = lax.axis_size("lev"), lax.axis_size("var")
    _, m_dev, x_all, y_all = ensemble.shape
    blocks, obs = obs_sites.shape
    tiles = tile_mask.shape[1]
    ens = ensemble.reshape(m_dev, x_all // 8, 8, y_all)
    here = (tiles, x_all // tiles, blocks, obs)
    cfg = (levels, count, 0, PARTS, *here)
    more_cfg = (levels, count, sum(PARTS), MORE_PARTS, *here)
    back, more = exchange(cfg, ens, obs_sites, owner, obs_values, obs_error)

    def with_more():
        more_back, _ = exchange(more_cfg, ens, obs_sites, owner, obs_values, obs_error)
        return apply((cfg, more_cfg), owner, ens, back, more_back)

    out = lax.cond(more[0] > 0, with_more, lambda: apply((cfg,), owner, ens, back))
    return out.reshape(ensemble.shape)


def solution(mesh):
    in_specs = (P("lev", "var", None, None), P(), P(), P(), P(), P())
    out_specs = P("lev", "var", None, None)
    return jax.shard_map(
        shards,
        mesh=mesh,
        in_specs=in_specs,
        out_specs=out_specs,
        check_vma=False,
    )
```

```python
import functools

import jax
import jax.numpy as jnp
from jax import lax
from jax.experimental import pallas as pl
from jax.experimental.pallas import tpu as pltpu
from jax.sharding import PartitionSpec as P

MESH = pl.DeviceIdType.MESH
HIGHEST = lax.Precision.HIGHEST
F32 = jnp.float32
REACH = 3
PARTS = (6, 8, 8)
MORE_PARTS = (6,)
VMEM_BYTES = 64 * 2**20
HALF = 64


def step_at(value, edge):
    return jnp.minimum(jnp.maximum(value - edge + 1, 0), 1)


def changed_tiles(owner_ref, blocks, tiles, start, slots):
    t = [owner_ref[b] & (tiles - 1) for b in range(blocks)]
    for i in range(blocks):
        for j in range(blocks - 1 - i):
            t[j], t[j + 1] = jnp.minimum(t[j], t[j + 1]), jnp.maximum(t[j], t[j + 1])
    befores, gaps, total, end = [], [], 0, -1
    for b in range(blocks):
        begin = jnp.maximum(jnp.maximum(t[b] - REACH, end + 1), 0)
        gaps.append(begin - end - 1)
        end = jnp.minimum(t[b] + REACH, tiles - 1)
        befores.append(total)
        total = total + jnp.maximum(end - begin + 1, 0)
    found = []
    for s in range(start, start + slots):
        tile = gaps[0] + s
        for b in range(1, blocks):
            tile = tile + gaps[b] * step_at(s, befores[b])
        found.append((tile + 1) * step_at(total - 1, s) - 1)
    return found, total


def places(parts, count):
    firsts = [sum(parts[:p]) for p in range(len(parts))]
    return firsts, [count * first for first in firsts]


def taper(dx, dy, radius):
    return jnp.square(jnp.maximum(0.0, 1.0 - (dx * dx + dy * dy) / (radius * radius)))


def exchange_kernel(
    cfg,
    sites_hbm,
    owner_hbm,
    values_hbm,
    errors_hbm,
    ens_ref,
    back_ref,
    more_hbm,
    sites_ref,
    owner_ref,
    values_ref,
    errors_ref,
    more_ref,
    ens_v,
    out_buf,
    in_buf,
    ret_buf,
    site_v,
    near_buf,
    row_buf,
    row_in,
    wcol_v,
    wcell_v,
    hcol_v,
    r_v,
    load_sem,
    small_sem,
    more_sem,
    near_send,
    near_recv,
    row_send,
    row_recv,
    bulk_send,
    bulk_recv,
    ret_send,
    ret_recv,
    own_sem,
):
    levels, count, start, parts, tiles, width, blocks, obs = cfg
    slots = sum(parts)
    n_obs = blocks * obs
    members = 2 * count
    lev = lax.axis_index("lev")
    me = lax.axis_index("var")
    radius = jnp.float32(REACH * width)
    tile_bits = tiles.bit_length() - 1
    firsts, bases = places(parts, count)

    load = pltpu.make_async_copy(ens_ref, ens_v, load_sem)
    small = [
        pltpu.make_async_copy(src, dst, small_sem.at[i])
        for i, (src, dst) in enumerate(
            [
                (owner_hbm, owner_ref),
                (sites_hbm, sites_ref),
                (values_hbm, values_ref),
                (errors_hbm, errors_ref),
            ]
        )
    ]
    for copy in small:
        copy.start()
    load.start()

    barrier = pltpu.get_barrier_semaphore()

    def greet(j, carry):
        pl.semaphore_signal(
            barrier, inc=1, device_id=(lev, lax.rem(me + j, count)), device_id_type=MESH
        )
        return carry

    lax.fori_loop(1, count, greet, 0)
    for j in range(1, levels):
        pl.semaphore_signal(
            barrier, inc=1, device_id=((lev + j) % levels, me), device_id_type=MESH
        )

    for copy in small:
        copy.wait()

    lane = lax.broadcasted_iota(jnp.int32, (1, 128), 1)
    low = lane < HALF
    tile_at, touched = changed_tiles(owner_ref, blocks, tiles, start, slots)
    more_ref[0] = step_at(touched - 1, start + slots)
    tell = pltpu.make_async_copy(more_ref, more_hbm, more_sem)
    tell.start()

    load.wait()

    for m in range(2):
        for i in range(n_obs):
            b, k = i // obs, i % obs
            site = sites_ref[b, k]
            away = (owner_ref[b] >> tile_bits) - lev
            row = ens_v[m, site >> 10, pl.ds((site >> 7) & 7, 1), :]
            site_v[pl.ds(m * n_obs + i, 1), :] = jnp.where(
                lane == (site & 127) + 128 * away, row, 0.0
            )
    sums = jnp.sum(site_v[...], axis=1, keepdims=True)
    sub64 = lax.broadcasted_iota(jnp.int32, (2 * n_obs, 128), 0)
    lane64 = lax.broadcasted_iota(jnp.int32, (2 * n_obs, 128), 1)
    mine = jnp.sum(jnp.where(sub64 == lane64, sums, 0.0), axis=0, keepdims=True)
    near_buf[pl.ds(0, 8), :] = jnp.broadcast_to(mine, (8, 128))

    pl.semaphore_wait(barrier, count - 1 + levels - 1)

    near = []
    for j in range(1, levels):
        copy = pltpu.make_async_remote_copy(
            near_buf.at[pl.ds(0, 8)],
            near_buf.at[pl.ds(8 * j, 8)],
            near_send.at[j],
            near_recv.at[j],
            device_id=((lev + j) % levels, me),
            device_id_type=MESH,
        )
        copy.start()
        near.append(copy)

    for p, size in enumerate(parts):
        for r in range(size):
            tile = jnp.maximum(tile_at[firsts[p] + r], 0)
            for g in range(4):
                a = ens_v[0, tile * (width // 8) + g]
                c = ens_v[1, tile * (width // 8) + g]
                row = bases[p] + g * 16 * size + r
                out_buf[pl.ds(row, 8, stride=size), :] = jnp.where(low, a, pltpu.roll(c, HALF, 1))
                out_buf[pl.ds(row + 8 * size, 8, stride=size), :] = jnp.where(
                    low, pltpu.roll(a, HALF, 1), c
                )

    def send_part(p, src, dst, send_sem, recv_sem):
        size = parts[p]

        def send(j, carry):
            to = lax.rem(me + j, count)
            pltpu.make_async_remote_copy(
                src.at[pl.ds(bases[p] + to * size, size)],
                dst.at[pl.ds(bases[p] + me * size, size)],
                send_sem.at[p],
                recv_sem.at[p],
                device_id=(lev, to),
                device_id_type=MESH,
            ).start()
            return carry

        lax.fori_loop(1, count, send, 0)

    def wait_part(p, buf, sem):
        rest = pl.ds(bases[p], (count - 1) * parts[p])
        pltpu.make_async_copy(buf.at[rest], buf.at[rest], sem.at[p]).wait()

    send_part(0, out_buf, in_buf, bulk_send, bulk_recv)
    for copy in near:
        copy.wait_recv()
    row_buf[...] = (near_buf[pl.ds(0, 8), :] + near_buf[pl.ds(8, 8), :]) + (
        near_buf[pl.ds(16, 8), :] + near_buf[pl.ds(24, 8), :]
    )

    def send_row(j, carry):
        to = lax.rem(me + j, count)
        pltpu.make_async_remote_copy(
            row_buf.at[pl.ds(0, 1)],
            row_in.at[pl.ds(me, 1)],
            row_send,
            row_recv,
            device_id=(lev, to),
            device_id_type=MESH,
        ).start()
        return carry

    lax.fori_loop(1, count, send_row, 0)
    for p in range(1, len(parts)):
        send_part(p, out_buf, in_buf, bulk_send, bulk_recv)
    row_in[pl.ds(me, 1), :] = row_buf[pl.ds(0, 1), :]
    for p, size in enumerate(parts):
        here = pl.ds(bases[p] + me * size, size)
        in_buf[here, :] = out_buf[here, :]
    sub32 = lax.broadcasted_iota(jnp.int32, (n_obs, 128), 0)
    lane32 = lax.broadcasted_iota(jnp.int32, (n_obs, 128), 1)
    site_c = jnp.zeros((n_obs, 128), jnp.int32)
    own_c = jnp.zeros((n_obs, 128), jnp.int32)
    err_c = jnp.zeros((n_obs, 128), F32)
    val_c = jnp.zeros((n_obs, 128), F32)
    site_r = jnp.zeros((1, 128), jnp.int32)
    own_r = jnp.zeros((1, 128), jnp.int32)
    for i in range(n_obs):
        b, k = i // obs, i % obs
        at = sub32 == i
        site_c = jnp.where(at, sites_ref[b, k], site_c)
        own_c = jnp.where(at, owner_ref[b], own_c)
        err_c = jnp.where(at, errors_ref[b, k], err_c)
        val_c = jnp.where(at, values_ref[b, k], val_c)
        site_r = jnp.where(lane == i, sites_ref[b, k], site_r)
        own_r = jnp.where(lane == i, owner_ref[b], own_r)
    x_c = (site_c >> 7).astype(F32)
    y_c = (site_c & 127).astype(F32)
    t_c = own_c & (tiles - 1)
    l_c = own_c >> tile_bits
    x_r = (site_r >> 7).astype(F32)
    y_r = (site_r & 127).astype(F32)
    t_r = own_r & (tiles - 1)
    l_r = own_r >> tile_bits
    pair_w = (
        jnp.where(jnp.abs(t_c - t_r) <= REACH, 1.0, 0.0)
        * jnp.exp2(-jnp.abs(l_c - l_r).astype(F32))
        * taper(x_c - x_r, y_c - y_r, radius)
    )
    row_w = jnp.where((lane32 > sub32) & (lane32 < n_obs), pair_w, 0.0)
    for k in range(n_obs):
        b = k // obs
        site = sites_ref[b, k % obs]
        own = owner_ref[b]
        w = (
            jnp.where(jnp.abs(t_c - (own & (tiles - 1))) <= REACH, 1.0, 0.0)
            * jnp.exp2(-jnp.abs(l_c - (own >> tile_bits)).astype(F32))
            * taper(x_c - (site >> 7).astype(F32), y_c - (site & 127).astype(F32), radius)
        )
        wcol_v[k] = jnp.where(sub32 > k, w, 0.0)

    group, side, column = me // 16, (me // 8) % 2, me % 8
    cell_y = (side * HALF + lane % HALF).astype(F32)
    level_f = jnp.exp2(-jnp.abs(l_c - lev).astype(F32))
    for p in range(slots // 2):
        tile = jnp.where(low, tile_at[2 * p], tile_at[2 * p + 1])
        cell_x = (tile * width + group * 8 + column).astype(F32)
        inside = (tile >= 0) & (jnp.abs(t_c - tile) <= REACH)
        wcell_v[p] = (
            jnp.where(inside, 1.0, 0.0) * level_f * taper(cell_x - x_c, cell_y - y_c, radius)
        )

    for copy in near:
        copy.wait_send()
    pltpu.make_async_copy(
        row_in.at[pl.ds(0, count - 1)], row_in.at[pl.ds(0, count - 1)], row_recv
    ).wait()

    raw = row_in[...]
    total = jnp.sum(raw, axis=0, keepdims=True)
    both = jnp.where(lane < n_obs, total + pltpu.roll(total, 128 - n_obs, 1), 0.0)
    mean_r = both / members
    mean2_r = mean_r + pltpu.roll(mean_r, n_obs, 1)
    centred = jnp.where(lane < 2 * n_obs, raw - mean2_r, 0.0)
    full = lax.dot_general(
        centred, centred, (((0,), (0,)), ((), ())), precision=HIGHEST, preferred_element_type=F32
    )
    gram = full[:n_obs] + pltpu.roll(full[n_obs : 2 * n_obs], 128 - n_obs, 1)
    gram = jnp.where(lane < n_obs, gram, 0.0)
    mean_c = jnp.sum(jnp.where(sub32 == lane32, mean_r, 0.0), axis=1, keepdims=True)
    mean_c = jnp.broadcast_to(mean_c, (n_obs, 128))
    mix = jnp.where(sub32 == lane32, 1.0, 0.0)
    alpha_c = jnp.zeros((n_obs, 128), F32)
    beta_c = jnp.zeros((n_obs, 128), F32)
    inv_c = jnp.zeros((n_obs, 128), F32)
    beta_r = jnp.zeros((1, 128), F32)
    for k in range(n_obs):
        u_row = gram[k : k + 1, :]
        u_col = jnp.broadcast_to(gram[:, k : k + 1], (n_obs, 128))
        d = u_col[k : k + 1, :]
        spread = d / (members - 1) + 1e-06
        r = err_c[k : k + 1, :]
        inv = 1.0 / (spread + r)
        alpha = spread * inv * (val_c[k : k + 1, :] - mean_c[k : k + 1, :])
        beta = jnp.sqrt(r * inv) - 1.0
        inv_scaled = 1.0 / ((members - 1) * spread)
        c_col = wcol_v[k] * u_col * inv_scaled
        g_row = row_w[k : k + 1, :] * u_row * (inv_scaled * beta)
        g_col = c_col * beta
        mean_c = mean_c + c_col * alpha
        gram = gram + (g_col * (u_row + g_row * d) + u_col * g_row)
        mix = mix + g_col * mix[k : k + 1, :]
        at = sub32 == k
        alpha_c = jnp.where(at, alpha, alpha_c)
        beta_c = jnp.where(at, beta, beta_c)
        inv_c = jnp.where(at, inv_scaled, inv_c)
        beta_r = jnp.where(lane == k, beta, beta_r)
    lower = jnp.where(lane32 < sub32, gram * beta_r, 0.0)
    for k in range(n_obs):
        hcol_v[k] = jnp.broadcast_to(lower[:, k : k + 1], (n_obs, 128))

    mix2 = jnp.concatenate([mix, pltpu.roll(mix, n_obs, 1)], axis=0)
    anomalies = lax.dot_general(
        mix2, centred, (((1,), (1,)), ((), ())), precision=HIGHEST, preferred_element_type=F32
    )
    shift = (
        jnp.concatenate([alpha_c, alpha_c], axis=0)[:, :count]
        + jnp.concatenate([beta_c, beta_c], axis=0)[:, :count] * anomalies
    )

    def half_sum(part):
        t = jnp.where(low, part[:n_obs], part[n_obs:])
        return t + pltpu.roll(t, HALF, 1)

    own = []
    for p, size in enumerate(parts):
        wait_part(p, in_buf, bulk_recv)
        for q in range(size // 2):
            row = bases[p] + 2 * q
            x = jnp.concatenate(
                [
                    in_buf[pl.ds(row, count, stride=size), :],
                    in_buf[pl.ds(row + 1, count, stride=size), :],
                ],
                axis=1,
            )
            r2 = jnp.dot(anomalies, x, precision=HIGHEST, preferred_element_type=F32)
            r_v[firsts[p] // 2 + q] = jnp.where(low, half_sum(r2[:, :128]), half_sum(r2[:, 128:]))

        for q in range(size // 2):
            row = bases[p] + 2 * q
            reg = r_v[firsts[p] // 2 + q]
            w = wcell_v[firsts[p] // 2 + q] * inv_c
            for k in range(n_obs - 1):
                reg = reg + hcol_v[k] * (w[k : k + 1, :] * reg[k : k + 1, :])
            coefs = w * reg
            turned = pltpu.roll(coefs, HALF, 1)
            zero = jnp.zeros_like(coefs)
            first = jnp.concatenate(
                [jnp.where(low, coefs, zero), jnp.where(low, zero, turned)], axis=0
            )
            second = jnp.concatenate(
                [jnp.where(low, turned, zero), jnp.where(low, zero, coefs)], axis=0
            )
            delta = lax.dot_general(
                shift,
                jnp.concatenate([first, second], axis=1),
                (((0,), (0,)), ((), ())),
                precision=HIGHEST,
                preferred_element_type=F32,
            )
            ret_buf[pl.ds(row, count, stride=size), :] = delta[:, :128]
            ret_buf[pl.ds(row + 1, count, stride=size), :] = delta[:, 128:]

        send_part(p, ret_buf, back_ref, ret_send, ret_recv)
        here = pl.ds(bases[p] + me * size, size)
        copy = pltpu.make_async_copy(ret_buf.at[here], back_ref.at[here], own_sem.at[p])
        copy.start()
        own.append(copy)

    tell.wait()
    rows = row_in.at[pl.ds(0, count - 1)]
    pltpu.make_async_copy(rows, rows, row_send).wait()
    for p in range(len(parts)):
        wait_part(p, out_buf, bulk_send)
        own[p].wait()
    for p in range(len(parts)):
        wait_part(p, back_ref, ret_recv)
    for p in range(len(parts)):
        wait_part(p, ret_buf, ret_send)


def apply_kernel(cfgs, owner_hbm, ens_ref, *refs):
    n = len(cfgs)
    backs, out_ref, owner_ref, ens_v, kept, sems = (
        refs[:n],
        refs[n],
        refs[n + 1],
        refs[n + 2],
        refs[n + 3 : 2 * n + 3],
        refs[2 * n + 3],
    )
    small = pltpu.make_async_copy(owner_hbm, owner_ref, sems.at[0])
    small.start()
    load_backs = [
        pltpu.make_async_copy(backs[i], kept[i], sems.at[5 + i]) for i in range(n)
    ]
    loads = [
        pltpu.make_async_copy(ens_ref.at[m], ens_v.at[m], sems.at[1 + m]) for m in range(2)
    ]
    for load in load_backs + loads:
        load.start()
    small.wait()
    low = lax.broadcasted_iota(jnp.int32, (1, 128), 1) < HALF
    for load in load_backs:
        load.wait()
    stores = []
    for m in range(2):
        loads[m].wait()
        for i, (levels, count, start, parts, tiles, width, blocks, obs) in enumerate(cfgs):
            firsts, bases = places(parts, count)
            tile_at, _ = changed_tiles(owner_ref, blocks, tiles, start, sum(parts))
            for p, size in enumerate(parts):
                for r in range(size):
                    tile = jnp.maximum(tile_at[firsts[p] + r], 0)
                    for g in range(4):
                        row = bases[p] + g * 16 * size + r
                        a = kept[i][pl.ds(row, 8, stride=size), :]
                        c = kept[i][pl.ds(row + 8 * size, 8, stride=size), :]
                        at = tile * (width // 8) + g
                        if m == 0:
                            added = jnp.where(low, a, pltpu.roll(c, HALF, 1))
                        else:
                            added = jnp.where(low, pltpu.roll(a, HALF, 1), c)
                        ens_v[m, at] = ens_v[m, at] + added
        store = pltpu.make_async_copy(ens_v.at[m], out_ref.at[m], sems.at[3 + m])
        store.start()
        stores.append(store)
    for store in stores:
        store.wait()


def exchange(cfg, ens, obs_sites, owner, obs_values, obs_error):
    levels, count, start, parts, tiles, width, blocks, obs = cfg
    slots = sum(parts)
    n_obs = blocks * obs
    hbm = pl.BlockSpec(memory_space=pltpu.HBM)
    anywhere = pl.BlockSpec(memory_space=pl.ANY)
    dma = pltpu.SemaphoreType.DMA
    limit = VMEM_BYTES - 4 * count * slots * 128
    return pl.pallas_call(
        functools.partial(exchange_kernel, cfg),
        out_shape=(
            jax.ShapeDtypeStruct((count * slots, 128), F32),
            jax.ShapeDtypeStruct((1,), jnp.int32),
        ),
        in_specs=[hbm] * 5,
        out_specs=(anywhere, hbm),
        scratch_shapes=[
            pltpu.SMEM(obs_sites.shape, jnp.int32),
            pltpu.SMEM(owner.shape, jnp.int32),
            pltpu.SMEM(obs_values.shape, F32),
            pltpu.SMEM(obs_error.shape, F32),
            pltpu.SMEM((1,), jnp.int32),
            pltpu.VMEM(ens.shape, F32),
            pltpu.VMEM((count * slots, 128), F32),
            pltpu.VMEM((count * slots, 128), F32),
            pltpu.VMEM((count * slots, 128), F32),
            pltpu.VMEM((2 * n_obs, 128), F32),
            pltpu.VMEM((8 * levels, 128), F32),
            pltpu.VMEM((8, 128), F32),
            pltpu.VMEM((count, 128), F32),
            pltpu.VMEM((n_obs, n_obs, 128), F32),
            pltpu.VMEM((slots // 2, n_obs, 128), F32),
            pltpu.VMEM((n_obs, n_obs, 128), F32),
            pltpu.VMEM((slots // 2, n_obs, 128), F32),
            dma,
            dma((4,)),
            dma,
            dma((levels,)),
            dma((levels,)),
            dma,
            dma,
            dma((len(parts),)),
            dma((len(parts),)),
            dma((len(parts),)),
            dma((len(parts),)),
            dma((len(parts),)),
        ],
        compiler_params=pltpu.CompilerParams(
            collective_id=1 + start, has_side_effects=True, vmem_limit_bytes=limit
        ),
    )(obs_sites, owner, obs_values, obs_error, ens)


def apply(cfgs, owner, ens, *backs):
    hbm = pl.BlockSpec(memory_space=pltpu.HBM)
    anywhere = pl.BlockSpec(memory_space=pl.ANY)
    dma = pltpu.SemaphoreType.DMA
    return pl.pallas_call(
        functools.partial(apply_kernel, cfgs),
        out_shape=jax.ShapeDtypeStruct(ens.shape, F32),
        in_specs=[hbm, hbm] + [anywhere] * len(backs),
        out_specs=hbm,
        scratch_shapes=[
            pltpu.SMEM(owner.shape, jnp.int32),
            pltpu.VMEM(ens.shape, F32),
            *[pltpu.VMEM(back.shape, F32) for back in backs],
            dma((5 + len(backs),)),
        ],
        compiler_params=pltpu.CompilerParams(
            vmem_limit_bytes=VMEM_BYTES - 4 * sum(back.size for back in backs)
        ),
    )(owner, ens, *backs)


def shards(ensemble, obs_sites, owner, tile_mask, obs_values, obs_error):
    levels, count = lax.axis_size("lev"), lax.axis_size("var")
    _, m_dev, x_all, y_all = ensemble.shape
    blocks, obs = obs_sites.shape
    tiles = tile_mask.shape[1]
    ens = ensemble.reshape(m_dev, x_all // 8, 8, y_all)
    here = (tiles, x_all // tiles, blocks, obs)
    cfg = (levels, count, 0, PARTS, *here)
    more_cfg = (levels, count, sum(PARTS), MORE_PARTS, *here)
    back, more = exchange(cfg, ens, obs_sites, owner, obs_values, obs_error)

    def with_more():
        more_back, _ = exchange(more_cfg, ens, obs_sites, owner, obs_values, obs_error)
        return apply((cfg, more_cfg), owner, ens, back, more_back)

    out = lax.cond(more[0] > 0, with_more, lambda: apply((cfg,), owner, ens, back))
    return out.reshape(ensemble.shape)


def solution(mesh):
    in_specs = (P("lev", "var", None, None), P(), P(), P(), P(), P())
    out_specs = P("lev", "var", None, None)
    return jax.shard_map(
        shards,
        mesh=mesh,
        in_specs=in_specs,
        out_specs=out_specs,
        check_vma=False,
    )
```
